32 devices in a mesh: view: 8 (over y, x, core), strip: 4 (over z).
Axes of the slice: x: 2, y: 2, z: 4, core: 2. Of those that a mesh axis runs over, the one named last changes fastest.
Arguments:
- tokens: bfloat16 [8, 512, 1536], P('view', 'strip'), may hold values from -48 to 48
- source_ids: int32 [8, 4, 5], replicated, may hold values from 0 to 31, as said below
- source_count: int32 [8, 4], replicated, may hold values from 2 to 5, as said below
- self_query: bfloat16 [1536, 1536], P(None, 'strip'), may hold values from -24 to 24
- self_key: bfloat16 [1536, 1536], P(None, 'strip'), may hold values from -24 to 24
- self_value: bfloat16 [1536, 1536], P(None, 'strip'), may hold values from -0.15625 to 0.15625
- self_out: bfloat16 [1536, 1536], P('strip'), may hold values from -1.1953125 to 1.1953125
- cross_query: bfloat16 [1536, 1536], P(None, 'strip'), may hold values from -24 to 24
- cross_key: bfloat16 [1536, 1536], P(None, 'strip'), may hold values from -24 to 24
- cross_value: bfloat16 [1536, 1536], P(None, 'strip'), may hold values from -0.15625 to 0.15625
- cross_out: bfloat16 [1536, 1536], P('strip'), may hold values from -1.1953125 to 1.1953125
- mlp_up: bfloat16 [1536, 6144], P(None, 'strip'), may hold values from -0.15625 to 0.15625
- mlp_down: bfloat16 [6144, 1536], P('strip'), may hold values from -0.078125 to 0.078125
Outputs:
- mixed: bfloat16 [8, 512, 1536], P('view', 'strip')
The draws below stay inside these ranges and needn't reach their ends.
Inputs may be any that keep to these rules, and one draw needn't show every extreme that they name: `source_ids`: entry k of strip s of view v names a strip of another view than v; entries with k >= source_count[v, s] are unused. Among all 20 entries of one destination view, used or not, each other view is named at most 3 times, and some view exactly 3 times. `source_count`: every view has a strip with all 5 entries in use.
All inputs are finite; a program needn't handle non-finite values.
Results may differ from the reference program's by a relative error of at most 0.015.
Values may be sent and summed in bfloat16 or wider, within the bound.
A program may use at most 128 MiB of HBM per device.

```python
import math
import jax
import jax.numpy as jnp
from jax import lax

D = 1536
HEADS = 24
HEAD_DIM = 64
FF = 6144
ROWS_DEV = 128
SLOTS = 5
VIEWS = 8
STRIPS = 4
VIEW_TOKENS = 512
CAP = 3


def draw_tokens(key, part):
    keys = jax.random.split(jax.random.fold_in(key, 7), 3)
    row_scale = jnp.exp(jax.random.uniform(keys[0], (VIEWS, VIEW_TOKENS, 1), jnp.float32, math.log(0.4), math.log(4.0)))
    col_scale = jnp.exp(jax.random.uniform(keys[1], (1, 1, D), jnp.float32, math.log(0.5), math.log(2.5)))
    base_part = jax.random.normal(keys[2], (VIEWS, VIEW_TOKENS, D), jnp.float32)
    return jnp.clip(base_part * row_scale * col_scale, -48.0, 48.0).astype(jnp.bfloat16)


def query_key_pair(key, salt_tag):
    keys = jax.random.split(jax.random.fold_in(key, salt_tag), 4)
    query_weight = jax.random.normal(keys[0], (D, D), jnp.float32) / math.sqrt(D)
    key_weight = jax.random.normal(keys[3], (D, D), jnp.float32) / math.sqrt(D)
    return (jnp.clip(query_weight, -24.0, 24.0), jnp.clip(key_weight, -24.0, 24.0))


def draw_self_query(key, part):
    return query_key_pair(key, 101)[0].astype(jnp.bfloat16)


def draw_self_key(key, part):
    return query_key_pair(key, 101)[1].astype(jnp.bfloat16)


def draw_cross_query(key, part):
    return query_key_pair(key, 202)[0].astype(jnp.bfloat16)


def draw_cross_key(key, part):
    return query_key_pair(key, 202)[1].astype(jnp.bfloat16)


def draw_source_ids(key, part):
    keys = jax.random.split(jax.random.fold_in(key, 303), 2)
    positions = (VIEWS - 1) * CAP
    view_keys = jax.random.split(keys[0], VIEWS)
    shuffled = jax.vmap(lambda one_key: jax.random.permutation(one_key, positions))(view_keys)
    entry_pos = shuffled[:, :STRIPS * SLOTS].astype(jnp.int32)
    offset = entry_pos // CAP
    dest_view = jnp.arange(VIEWS, dtype=jnp.int32)[:, None]
    source_view = (dest_view + 1 + offset) % VIEWS
    source_strip = jax.random.randint(keys[1], (VIEWS, STRIPS * SLOTS), 0, STRIPS, jnp.int32)
    return (source_view * STRIPS + source_strip).reshape(VIEWS, STRIPS, SLOTS).astype(jnp.int32)


def draw_source_count(key, part):
    keys = jax.random.split(jax.random.fold_in(key, 404), 2)
    counted = jax.random.randint(keys[0], (VIEWS, STRIPS), 2, SLOTS + 1, jnp.int32)
    full_strip = jax.random.randint(keys[1], (VIEWS, 1), 0, STRIPS, jnp.int32)
    strip_index = jnp.arange(STRIPS, dtype=jnp.int32)[None, :]
    return jnp.where(strip_index == full_strip, SLOTS, counted).astype(jnp.int32)


def block_levels(stream_key, extent, shards, low, largest):
    def one(axis_at, parts):
        draws = jax.random.uniform(jax.random.fold_in(jax.random.fold_in(stream_key, 6), axis_at), (parts,), jnp.float32, low / len(shards), largest / len(shards))
        return jnp.repeat(jnp.exp(draws), extent[axis_at] // parts).reshape((-1,) + (1,) * (len(extent) - axis_at - 1))

    level = one(*shards[0])
    for cut in shards[1:]:
        level = level * one(*cut)
    return level


def gaussian(own_key, extent, deviation, reach, cuts=(), held_as=jnp.bfloat16):
    factor_of = block_levels(own_key, extent, cuts, -0.22, 0.18) if cuts else 1.0
    entries = jax.random.normal(own_key, extent, jnp.float32) * deviation * factor_of
    return jnp.minimum(jnp.maximum(entries, -reach), reach).astype(held_as)


def setup_inputs(seed: int = 0) -> dict:
    key_list = jax.random.split(jax.random.key(seed), 14)
    return {
        "tokens": draw_tokens(jax.random.fold_in(key_list[13], 71), 0),
        "source_ids": draw_source_ids(jax.random.fold_in(key_list[13], 71), 0),
        "source_count": draw_source_count(jax.random.fold_in(key_list[13], 71), 0),
        "self_query": draw_self_query(jax.random.fold_in(key_list[13], 71), 0),
        "self_key": draw_self_key(jax.random.fold_in(key_list[13], 71), 0),
        "self_value": gaussian(key_list[5], (D, D), D ** -0.5, 0.15625, ((1, 4),)),
        "self_out": gaussian(key_list[6], (D, D), 0.2, 1.1953125, ((0, 4),)),
        "cross_query": draw_cross_query(jax.random.fold_in(key_list[13], 71), 0),
        "cross_key": draw_cross_key(jax.random.fold_in(key_list[13], 71), 0),
        "cross_value": gaussian(key_list[9], (D, D), D ** -0.5, 0.15625, ((1, 4),)),
        "cross_out": gaussian(key_list[10], (D, D), 0.2, 1.1953125, ((0, 4),)),
        "mlp_up": gaussian(key_list[11], (D, FF), D ** -0.5, 0.15625, ((1, 4),)),
        "mlp_down": gaussian(key_list[12], (FF, D), FF ** -0.5, 0.078125, ((0, 4),)),
    }


def rms_rows(values_in):
    widened = values_in.astype(jnp.float32)
    scaled = widened * lax.rsqrt(lax.optimization_barrier(jnp.mean(widened * widened, axis=-1, keepdims=True)) + 1e-06)
    return scaled.astype(jnp.bfloat16)

def project_bf(normed, weight):
    return jnp.dot(normed, weight, preferred_element_type=jnp.float32).astype(jnp.bfloat16)

def attend_heads(query_heads, key_heads, value_heads, key_mask):
    scale = 1.0 / math.sqrt(HEAD_DIM)
    scores = jnp.einsum('qhe,khe->hqk', query_heads.astype(jnp.float32), key_heads.astype(jnp.float32)) * scale
    scores = jnp.where(key_mask[None, None, :], scores, -1e+30)
    weights = jax.nn.softmax(scores, axis=-1).astype(jnp.bfloat16)
    mixed_heads = jnp.einsum('hqk,khe->qhe', weights.astype(jnp.float32), value_heads.astype(jnp.float32))
    return mixed_heads.reshape(mixed_heads.shape[0], -1).astype(jnp.bfloat16)

def reference(tokens, source_ids, source_count, self_query, self_key, self_value, self_out, cross_query, cross_key, cross_value, cross_out, mlp_up, mlp_down):
    normed_all = rms_rows(tokens)
    cross_keys_all = lax.map(lambda view_rows: project_bf(view_rows, cross_key), normed_all).reshape(VIEWS * STRIPS, ROWS_DEV, D)
    cross_values_all = lax.map(lambda view_rows: project_bf(view_rows, cross_value), normed_all).reshape(VIEWS * STRIPS, ROWS_DEV, D)
    slot_index = jnp.arange(SLOTS).astype(jnp.int32)

    def one_view(view_index):
        view_rows = normed_all[view_index]
        head_shape = (VIEW_TOKENS, HEADS, HEAD_DIM)
        self_mix = attend_heads(project_bf(view_rows, self_query).reshape(head_shape), project_bf(view_rows, self_key).reshape(head_shape), project_bf(view_rows, self_value).reshape(head_shape), jnp.ones((VIEW_TOKENS,), dtype=bool))
        entry_ids = source_ids[view_index].reshape(-1).astype(jnp.int32)
        picked_keys = cross_keys_all[entry_ids].reshape(STRIPS, SLOTS * ROWS_DEV, HEADS, HEAD_DIM)
        picked_values = cross_values_all[entry_ids].reshape(STRIPS, SLOTS * ROWS_DEV, HEADS, HEAD_DIM)
        key_valid = jnp.repeat(slot_index[None, :] < source_count[view_index][:, None], ROWS_DEV, axis=1)
        cross_heads = project_bf(view_rows, cross_query).reshape(STRIPS, ROWS_DEV, HEADS, HEAD_DIM)
        cross_mix = jax.vmap(attend_heads)(cross_heads, picked_keys, picked_values, key_valid).reshape(VIEW_TOKENS, D)
        hidden = jax.nn.gelu(jnp.dot(view_rows, mlp_up, preferred_element_type=jnp.float32)).astype(jnp.bfloat16)
        branch_total = jnp.dot(self_mix, self_out, preferred_element_type=jnp.float32)
        branch_total = branch_total + jnp.dot(cross_mix, cross_out, preferred_element_type=jnp.float32)
        branch_total = branch_total + jnp.dot(hidden, mlp_down, preferred_element_type=jnp.float32)
        return (tokens[view_index].astype(jnp.float32) + branch_total).astype(jnp.bfloat16)
    return lax.map(one_view, jnp.arange(VIEWS).astype(jnp.int32))
```

```python
import functools
import math

import jax
import jax.numpy as jnp
from jax import lax
from jax.experimental import pallas as pl
from jax.experimental.pallas import tpu as pltpu
from jax.sharding import PartitionSpec as P

HEAD_DIM = 64
LANES = 128
MESH = pl.DeviceIdType.MESH
F32 = jnp.float32
BF16 = jnp.bfloat16


def dot(a, b):
    return jnp.dot(a, b, preferred_element_type=F32)


def dot_nt(a, b):
    return lax.dot_general(a, b, (((1,), (1,)), ((), ())), preferred_element_type=F32)


def attend(q, keys, values, bias):
    cols = q.shape[1]
    parts = []
    for lo in range(0, cols, LANES):
        hi = min(lo + LANES, cols)
        q_block = q[:, lo:hi] * jnp.asarray(1.0 / math.sqrt(HEAD_DIM), BF16)
        k_block, v_block = keys(lo, hi), values(lo, hi)
        lane = lax.broadcasted_iota(jnp.int32, q_block.shape, 1)
        result = None
        for head in range((hi - lo) // HEAD_DIM):
            inside = jnp.logical_and(lane >= head * HEAD_DIM, lane < (head + 1) * HEAD_DIM)
            scores = dot_nt(jnp.where(inside, q_block, jnp.zeros_like(q_block)), k_block)
            if bias is not None:
                scores = scores + bias
            top = jnp.max(scores, axis=-1, keepdims=True)
            weights = jnp.exp(scores - top)
            total = jnp.sum(weights, axis=-1, keepdims=True)
            mixed = dot(weights.astype(BF16), v_block) * (1.0 / total)
            result = mixed if result is None else jnp.where(inside, mixed, result)
        parts.append(result.astype(BF16))
    return parts[0] if len(parts) == 1 else jnp.concatenate(parts, axis=1)


def kernel(
    n_view,
    n_strip,
    slots,
    ids,
    counts,
    tokens,
    w_sq,
    w_sk,
    w_sv,
    w_so,
    w_cq,
    w_ck,
    w_cv,
    w_co,
    w_up,
    w_down,
    out,
    wa,
    wo,
    wm,
    md,
    nbuf,
    proj,
    kv,
    kbuf,
    acc,
    rs_send,
    rs_recv,
    w_sem,
    n_send,
    n_recv,
    kv_send,
    fwd_send,
    kv_recv,
    rs_ssem,
    rs_rsem,
):
    v = lax.axis_index("view")
    z = lax.axis_index("strip")
    n_chip = n_view // 2
    chip, core = v // 2, v % 2
    mate = chip * 2 + 1 - core
    rows = tokens.shape[1]
    hc = w_sq.shape[1]
    n_up, _, up = wm.shape
    has_left, has_right = z > 0, z < n_strip - 1

    loads = []

    def load(src, dst):
        copy = pltpu.make_async_copy(src, dst, w_sem.at[len(loads)])
        copy.start()
        loads.append(copy)

    load(w_ck, wa.at[4])
    load(w_cv, wa.at[5])
    load(w_sq, wa.at[0])
    load(w_sk, wa.at[1])
    load(w_sv, wa.at[2])
    load(w_cq, wa.at[3])
    for j in range(n_up):
        load(w_up.at[:, pl.ds(j * up, up)], wm.at[j])
    for j in range(n_up):
        load(w_down.at[pl.ds(j * up, up)], md.at[j])
    load(w_so, wo.at[0])
    load(w_co, wo.at[1])

    barrier = pltpu.get_barrier_semaphore()

    def greet(view, strip):
        pl.semaphore_signal(barrier, inc=1, device_id=(view, strip), device_id_type=MESH)

    peers = [lax.rem(chip + o, n_chip) * 2 + core for o in range(1, n_chip)]
    for p in peers:
        greet(p, z)
    greet(mate, z)

    @pl.when(has_left)
    def _():
        greet(v, z - 1)

    @pl.when(has_right)
    def _():
        greet(v, z + 1)

    wide = tokens[0].astype(F32)
    nbuf[z] = (wide * lax.rsqrt(jnp.mean(wide * wide, axis=-1, keepdims=True) + 1e-06)).astype(BF16)
    pl.semaphore_wait(
        barrier, n_chip + jnp.where(has_left, 1, 0) + jnp.where(has_right, 1, 0)
    )

    def n_copy(b, side):
        return pltpu.make_async_remote_copy(
            src_ref=nbuf.at[b],
            dst_ref=nbuf.at[b],
            send_sem=n_send.at[side, b],
            recv_sem=n_recv.at[b],
            device_id=(v, z + (2 * side - 1)),
            device_id_type=MESH,
        )

    def kv_copy(view, t, to, sem):
        index = view * n_strip + t
        return pltpu.make_async_remote_copy(
            src_ref=kv.at[index],
            dst_ref=kv.at[index],
            send_sem=sem,
            recv_sem=kv_recv.at[index],
            device_id=(to, z),
            device_id_type=MESH,
        )

    def share(t):
        for o, p in enumerate(peers):
            kv_copy(v, t, p, kv_send.at[o, t]).start()
        kv_copy(v, t, mate, kv_send.at[n_chip - 1, t]).start()

    def forward(t):
        for o, p in enumerate(peers):
            kv_copy(p, t, mate, fwd_send.at[o, t]).wait_recv()
            kv_copy(p, t, mate, fwd_send.at[o, t]).start()

    def project_kv(b):
        x = nbuf[b]
        index = v * n_strip + b
        kv[index, :, 0:hc] = dot(x, wa[4]).astype(BF16)
        kv[index, :, hc : 2 * hc] = dot(x, wa[5]).astype(BF16)
        share(b)

    def project_rest(b):
        def one(i, carry):
            proj[i, b] = dot(nbuf[b], wa[i]).astype(BF16)
            return carry

        lax.fori_loop(0, 4, one, 0)

        def mlp(j, carry):
            hidden = jax.nn.gelu(dot(nbuf[b], wm[j])).astype(BF16)
            term = dot(hidden, md[j])

            @pl.when(j == 0)
            def _():
                acc[b] = term

            @pl.when(j > 0)
            def _():
                acc[b] = acc[b] + term

            return carry

        lax.fori_loop(0, n_up, mlp, 0)

    def at_distance(d, fn):
        @pl.when(z - d >= 0)
        def _():
            fn(z - d)

        @pl.when(z + d < n_strip)
        def _():
            fn(z + d)

    @pl.when(has_left)
    def _():
        n_copy(z, 0).start()

    @pl.when(has_right)
    def _():
        n_copy(z, 1).start()

    for copy in loads[:2]:
        copy.wait()
    project_kv(z)
    for copy in loads[2:]:
        copy.wait()
    project_rest(z)

    def gather_step(d, carry):
        @pl.when(z - d >= 0)
        def _():
            n_copy(z - d, 1).wait_recv()

            @pl.when(has_right)
            def _():
                n_copy(z - d, 1).start()

        @pl.when(z + d < n_strip)
        def _():
            n_copy(z + d, 0).wait_recv()

            @pl.when(has_left)
            def _():
                n_copy(z + d, 0).start()

        def both(fn):
            def one(side, c):
                b = z + (2 * side - 1) * d

                @pl.when(jnp.logical_and(b >= 0, b < n_strip))
                def _():
                    fn(b)

                return c

            lax.fori_loop(0, 2, one, 0)

        both(project_kv)
        both(project_rest)

        @pl.when(d == 1)
        def _():
            forward(z)

        @pl.when(d > 1)
        def _():
            both_prev = d - 1
            at_distance(both_prev, forward)

        return carry

    lax.fori_loop(1, n_strip, gather_step, 0)

    def self_strip(s, carry):
        def columns(i):
            return lambda lo, hi: proj[i, :, :, lo:hi].reshape(n_strip * rows, hi - lo)

        mixed = attend(proj[0, s], columns(1), columns(2), None)
        acc[s] = acc[s] + dot(mixed, wo[0])
        return carry

    lax.fori_loop(0, n_strip, self_strip, 0)

    at_distance(n_strip - 1, forward)

    def from_mate(t, carry):
        kv_copy(mate, t, mate, fwd_send.at[0, t]).wait_recv()
        for p in peers:
            kv_copy(p + 1 - 2 * core, t, mate, fwd_send.at[0, t]).wait_recv()
        return carry

    lax.fori_loop(0, n_strip, from_mate, 0)

    def rs_copy(s, side):
        slot = jnp.where(jnp.logical_and(side == 0, s == z - 1), n_strip, s)
        return pltpu.make_async_remote_copy(
            src_ref=rs_send.at[s],
            dst_ref=rs_recv.at[slot],
            send_sem=rs_ssem.at[s],
            recv_sem=rs_rsem.at[slot],
            device_id=(v, z + (2 * side - 1)),
            device_id_type=MESH,
        )

    def rs_wait(slot, side):
        pltpu.make_async_remote_copy(
            src_ref=rs_send.at[0],
            dst_ref=rs_recv.at[slot],
            send_sem=rs_ssem.at[0],
            recv_sem=rs_rsem.at[slot],
            device_id=(v, z + (2 * side - 1)),
            device_id_type=MESH,
        ).wait_recv()

    def nth(i):
        low = n_strip - 1 - i
        low = jnp.where(low > z, low, low - 1)
        high = jnp.where(i < z, i, i + 1)
        return jnp.where(i == n_strip - 1, z, jnp.where(z < n_strip // 2, low, high))

    def cross_strip(i, carry):
        s = nth(i)
        base = (v * n_strip + s) * slots
        for k in range(slots):
            kbuf[k] = kv[ids[base + k]]
        count = counts[v * n_strip + s]
        column = lax.broadcasted_iota(jnp.int32, (1, slots * rows), 1)
        bias = jnp.where(column < count * rows, 0.0, -1e30).astype(F32)

        def columns(start):
            return lambda lo, hi: kbuf[:, :, start + lo : start + hi].reshape(slots * rows, hi - lo)

        mixed = attend(proj[3, s], columns(0), columns(hc), bias)
        acc[s] = acc[s] + dot(mixed, wo[1])

        @pl.when(jnp.logical_and(s > z, z == 0))
        def _():
            rs_send[s] = acc[s].astype(BF16)
            rs_copy(s, 1).start()

        @pl.when(jnp.logical_and(s < z, z == n_strip - 1))
        def _():
            rs_send[s] = acc[s].astype(BF16)
            rs_copy(s, 0).start()

        return carry

    lax.fori_loop(0, n_strip, cross_strip, 0)

    def pass_on(i, carry):
        s = nth(i)

        @pl.when(jnp.logical_and(s > z, has_left))
        def _():
            rs_wait(s, 1)
            rs_send[s] = (acc[s] + rs_recv[s].astype(F32)).astype(BF16)
            rs_copy(s, 1).start()

        @pl.when(jnp.logical_and(s < z, has_right))
        def _():
            rs_wait(s, 0)
            rs_send[s] = (acc[s] + rs_recv[s].astype(F32)).astype(BF16)
            rs_copy(s, 0).start()

        return carry

    lax.fori_loop(0, n_strip - 1, pass_on, 0)

    @pl.when(has_left)
    def _():
        rs_wait(z, 1)
        acc[z] = acc[z] + rs_recv[z].astype(F32)

    @pl.when(has_right)
    def _():
        rs_wait(n_strip, 0)
        acc[z] = acc[z] + rs_recv[n_strip].astype(F32)

    out[0] = (tokens[0].astype(F32) + acc[z]).astype(BF16)

    def settle(t, carry):
        @pl.when(jnp.logical_and(has_left, t >= z))
        def _():
            n_copy(t, 0).wait_send()

        @pl.when(jnp.logical_and(has_right, t <= z))
        def _():
            n_copy(t, 1).wait_send()

        for o, p in enumerate(peers):
            kv_copy(v, t, p, kv_send.at[o, t]).wait_send()
            kv_copy(p, t, mate, fwd_send.at[o, t]).wait_send()
        kv_copy(v, t, mate, kv_send.at[n_chip - 1, t]).wait_send()

        @pl.when(t > z)
        def _():
            rs_copy(t, 1).wait_send()

        @pl.when(t < z)
        def _():
            rs_copy(t, 0).wait_send()

        return carry

    lax.fori_loop(0, n_strip, settle, 0)


def per_device(n_view, n_strip, tokens, source_ids, source_count, *weights):
    rows, width = tokens.shape[1:]
    hc = weights[0].shape[1]
    hidden = weights[-2].shape[1]
    slots = source_ids.shape[2]
    up = next(u for u in (384, 256, 128, hidden) if hidden % u == 0)
    n_up = hidden // up
    n_chip = n_view // 2
    dma = pltpu.SemaphoreType.DMA
    smem = pl.BlockSpec(memory_space=pltpu.SMEM)
    vmem = pl.BlockSpec(memory_space=pltpu.VMEM)
    hbm = pl.BlockSpec(memory_space=pl.ANY)
    return pl.pallas_call(
        functools.partial(kernel, n_view, n_strip, slots),
        out_shape=jax.ShapeDtypeStruct(tokens.shape, tokens.dtype),
        in_specs=[smem, smem, vmem] + [hbm] * len(weights),
        out_specs=vmem,
        scratch_shapes=[
            pltpu.VMEM((6, width, hc), BF16),
            pltpu.VMEM((2, hc, width), BF16),
            pltpu.VMEM((n_up, width, up), BF16),
            pltpu.VMEM((n_up, up, width), BF16),
            pltpu.VMEM((n_strip, rows, width), BF16),
            pltpu.VMEM((4, n_strip, rows, hc), BF16),
            pltpu.VMEM((n_view * n_strip, rows, 2 * hc), BF16),
            pltpu.VMEM((slots, rows, 2 * hc), BF16),
            pltpu.VMEM((n_strip, rows, width), F32),
            pltpu.VMEM((n_strip, rows, width), BF16),
            pltpu.VMEM((n_strip + 1, rows, width), BF16),
            dma((8 + 2 * n_up,)),
            dma((2, n_strip)),
            dma((n_strip,)),
            dma((n_chip, n_strip)),
            dma((n_chip, n_strip)),
            dma((n_view * n_strip,)),
            dma((n_strip,)),
            dma((n_strip + 1,)),
        ],
        compiler_params=pltpu.CompilerParams(
            collective_id=0, has_side_effects=True, vmem_limit_bytes=60 * 1024 * 1024
        ),
    )(source_ids.reshape(-1), source_count.reshape(-1), tokens, *weights)


def solution(mesh):
    column, row = P(None, "strip"), P("strip", None)
    in_specs = (
        P("view", "strip", None),
        P(),
        P(),
        column,
        column,
        column,
        row,
        column,
        column,
        column,
        row,
        column,
        row,
    )
    return jax.shard_map(
        functools.partial(per_device, mesh.shape["view"], mesh.shape["strip"]),
        mesh=mesh,
        in_specs=in_specs,
        out_specs=P("view", "strip", None),
        check_vma=False,
    )
```

```python
import functools
import math

import jax
import jax.numpy as jnp
from jax import lax
from jax.experimental import pallas as pl
from jax.experimental.pallas import tpu as pltpu
from jax.sharding import PartitionSpec as P

HEAD_DIM = 64
LANES = 128
MESH = pl.DeviceIdType.MESH
F32 = jnp.float32
BF16 = jnp.bfloat16


def dot(a, b):
    return jnp.dot(a, b, preferred_element_type=F32)


def dot_nt(a, b):
    return lax.dot_general(a, b, (((1,), (1,)), ((), ())), preferred_element_type=F32)


def attend(q, keys, values, bias):
    cols = q.shape[1]
    parts = []
    for lo in range(0, cols, LANES):
        hi = min(lo + LANES, cols)
        q_block = q[:, lo:hi] * jnp.asarray(1.0 / math.sqrt(HEAD_DIM), BF16)
        k_block, v_block = keys(lo, hi), values(lo, hi)
        lane = lax.broadcasted_iota(jnp.int32, q_block.shape, 1)
        result = None
        for head in range((hi - lo) // HEAD_DIM):
            inside = jnp.logical_and(lane >= head * HEAD_DIM, lane < (head + 1) * HEAD_DIM)
            scores = dot_nt(jnp.where(inside, q_block, jnp.zeros_like(q_block)), k_block)
            if bias is not None:
                scores = scores + bias
            top = jnp.max(scores, axis=-1, keepdims=True)
            weights = jnp.exp(scores - top)
            total = jnp.sum(weights, axis=-1, keepdims=True)
            mixed = dot(weights.astype(BF16), v_block) * (1.0 / total)
            result = mixed if result is None else jnp.where(inside, mixed, result)
        parts.append(result.astype(BF16))
    return parts[0] if len(parts) == 1 else jnp.concatenate(parts, axis=1)


def kernel(
    n_view,
    n_strip,
    slots,
    ids_in,
    counts_in,
    tokens,
    w_sq,
    w_sk,
    w_sv,
    w_so,
    w_cq,
    w_ck,
    w_cv,
    w_co,
    w_up,
    w_down,
    out,
    ids,
    counts,
    wa,
    wo,
    wm,
    md,
    nbuf,
    proj,
    kv,
    kbuf,
    acc,
    rs_send,
    rs_recv,
    w_sem,
    n_send,
    n_recv,
    kv_send,
    fwd_send,
    rel_send,
    kv_recv,
    rs_ssem,
    rs_rsem,
):
    v = lax.axis_index("view")
    z = lax.axis_index("strip")
    n_chip = n_view // 2
    chip, core = v // 2, v % 2
    mate = chip * 2 + 1 - core
    rows = tokens.shape[1]
    hc = w_sq.shape[1]
    n_up, _, up = wm.shape
    has_left, has_right = z > 0, z < n_strip - 1

    loads = []

    def load(src, dst):
        copy = pltpu.make_async_copy(src, dst, w_sem.at[len(loads)])
        copy.start()
        loads.append(copy)

    load(w_ck, wa.at[4])
    load(w_cv, wa.at[5])

    barrier = pltpu.get_barrier_semaphore()

    def greet(view, strip):
        pl.semaphore_signal(barrier, inc=1, device_id=(view, strip), device_id_type=MESH)

    relay = n_chip == 4
    if relay:
        near_x = chip + 1 - 2 * (chip % 2)
        near_y = lax.rem(chip + 2, 4)
        peers = [near_x * 2 + core, near_y * 2 + core]
        far = lax.rem(near_x + 2, 4) * 2 + core
        others = peers + [far]
    else:
        peers = [lax.rem(chip + o, n_chip) * 2 + core for o in range(1, n_chip)]
        others = peers
    for p in peers:
        greet(p, z)
    greet(mate, z)

    @pl.when(has_left)
    def _():
        greet(v, z - 1)

    @pl.when(has_right)
    def _():
        greet(v, z + 1)

    wide = tokens[0].astype(F32)
    nbuf[z] = (wide * lax.rsqrt(jnp.mean(wide * wide, axis=-1, keepdims=True) + 1e-06)).astype(BF16)
    pl.semaphore_wait(
        barrier, len(peers) + 1 + jnp.where(has_left, 1, 0) + jnp.where(has_right, 1, 0)
    )

    def n_copy(b, side):
        return pltpu.make_async_remote_copy(
            src_ref=nbuf.at[b],
            dst_ref=nbuf.at[b],
            send_sem=n_send.at[side, b],
            recv_sem=n_recv.at[b],
            device_id=(v, z + (2 * side - 1)),
            device_id_type=MESH,
        )

    def kv_copy(view, t, to, sem, half=None):
        index = view * n_strip + t
        part = kv.at[index]
        if half is not None:
            part = kv.at[index, pl.ds(half * (rows // 2), rows // 2)]
        return pltpu.make_async_remote_copy(
            src_ref=part,
            dst_ref=part,
            send_sem=sem,
            recv_sem=kv_recv.at[index, half or 0],
            device_id=(to, z),
            device_id_type=MESH,
        )

    def share(t):
        for o, p in enumerate(peers):
            kv_copy(v, t, p, kv_send.at[o, t]).start()
        kv_copy(v, t, mate, kv_send.at[n_chip - 1, t]).start()

    def forward(t):
        for o, p in enumerate(peers):
            kv_copy(p, t, mate, fwd_send.at[o, t]).wait_recv()
            if relay:
                kv_copy(p, t, peers[1 - o], rel_send.at[o, t], o).start()
            kv_copy(p, t, mate, fwd_send.at[o, t]).start()

    def forward_far(t):
        if relay:
            for half in range(2):
                kv_copy(far, t, mate, fwd_send.at[2, t], half).wait_recv()
            kv_copy(far, t, mate, fwd_send.at[2, t]).start()

    def project_kv(b):
        x = nbuf[b]
        index = v * n_strip + b
        kv[index, :, 0:hc] = dot(x, wa[4]).astype(BF16)
        kv[index, :, hc : 2 * hc] = dot(x, wa[5]).astype(BF16)
        share(b)

    def project_rest(b):
        def one(i, carry):
            proj[i, b] = dot(nbuf[b], wa[i]).astype(BF16)
            return carry

        lax.fori_loop(0, 4, one, 0)

        def mlp(j, carry):
            hidden = jax.nn.gelu(dot(nbuf[b], wm[j])).astype(BF16)
            term = dot(hidden, md[j])

            @pl.when(j == 0)
            def _():
                acc[b] = term

            @pl.when(j > 0)
            def _():
                acc[b] = acc[b] + term

            return carry

        lax.fori_loop(0, n_up, mlp, 0)

    def at_distance(d, fn):
        @pl.when(z - d >= 0)
        def _():
            fn(z - d)

        @pl.when(jnp.logical_and(z + d < n_strip, d > 0))
        def _():
            fn(z + d)

    @pl.when(has_left)
    def _():
        n_copy(z, 0).start()

    @pl.when(has_right)
    def _():
        n_copy(z, 1).start()

    load(w_sq, wa.at[0])
    load(w_sk, wa.at[1])
    load(w_sv, wa.at[2])
    load(w_cq, wa.at[3])
    for j in range(n_up):
        load(w_up.at[:, pl.ds(j * up, up)], wm.at[j])
    for j in range(n_up):
        load(w_down.at[pl.ds(j * up, up)], md.at[j])
    load(w_so, wo.at[0])
    load(w_co, wo.at[1])
    load(ids_in, ids)
    load(counts_in, counts)

    for copy in loads[:2]:
        copy.wait()
    project_kv(z)
    for copy in loads[2:]:
        copy.wait()
    project_rest(z)

    def gather_step(d, carry):
        @pl.when(z - d >= 0)
        def _():
            n_copy(z - d, 1).wait_recv()

            @pl.when(has_right)
            def _():
                n_copy(z - d, 1).start()

        @pl.when(z + d < n_strip)
        def _():
            n_copy(z + d, 0).wait_recv()

            @pl.when(has_left)
            def _():
                n_copy(z + d, 0).start()

        def both(fn):
            def one(side, c):
                b = z + (2 * side - 1) * d

                @pl.when(jnp.logical_and(b >= 0, b < n_strip))
                def _():
                    fn(b)

                return c

            lax.fori_loop(0, 2, one, 0)

        both(project_kv)
        at_distance(d - 1, forward)
        both(project_rest)
        at_distance(d - 1, forward_far)
        return carry

    lax.fori_loop(1, n_strip, gather_step, 0)
    at_distance(n_strip - 1, forward)

    def self_strip(s, carry):
        def columns(i):
            return lambda lo, hi: proj[i, :, :, lo:hi].reshape(n_strip * rows, hi - lo)

        mixed = attend(proj[0, s], columns(1), columns(2), None)
        acc[s] = acc[s] + dot(mixed, wo[0])
        return carry

    lax.fori_loop(0, n_strip, self_strip, 0)

    at_distance(n_strip - 1, forward_far)

    def from_mate(t, carry):
        kv_copy(mate, t, mate, fwd_send.at[0, t]).wait_recv()
        for p in others:
            kv_copy(p + 1 - 2 * core, t, mate, fwd_send.at[0, t]).wait_recv()
        return carry

    lax.fori_loop(0, n_strip, from_mate, 0)

    def rs_copy(s, side):
        slot = jnp.where(jnp.logical_and(side == 0, s == z - 1), n_strip, s)
        return pltpu.make_async_remote_copy(
            src_ref=rs_send.at[s],
            dst_ref=rs_recv.at[slot],
            send_sem=rs_ssem.at[s],
            recv_sem=rs_rsem.at[slot],
            device_id=(v, z + (2 * side - 1)),
            device_id_type=MESH,
        )

    def rs_wait(slot, side):
        pltpu.make_async_remote_copy(
            src_ref=rs_send.at[0],
            dst_ref=rs_recv.at[slot],
            send_sem=rs_ssem.at[0],
            recv_sem=rs_rsem.at[slot],
            device_id=(v, z + (2 * side - 1)),
            device_id_type=MESH,
        ).wait_recv()

    def nth(i):
        low = n_strip - 1 - i
        low = jnp.where(low > z, low, low - 1)
        high = jnp.where(i < z, i, i + 1)
        return jnp.where(i == n_strip - 1, z, jnp.where(z < n_strip // 2, low, high))

    def cross_strip(i, carry):
        s = nth(i)
        for k in range(slots):
            kbuf[k] = kv[ids[k, s, v]]
        count = counts[s, v]
        column = lax.broadcasted_iota(jnp.int32, (1, slots * rows), 1)
        bias = jnp.where(column < count * rows, 0.0, -1e30).astype(F32)

        def columns(start):
            return lambda lo, hi: kbuf[:, :, start + lo : start + hi].reshape(slots * rows, hi - lo)

        mixed = attend(proj[3, s], columns(0), columns(hc), bias)
        acc[s] = acc[s] + dot(mixed, wo[1])

        @pl.when(jnp.logical_and(s > z, z == 0))
        def _():
            rs_send[s] = acc[s].astype(BF16)
            rs_copy(s, 1).start()

        @pl.when(jnp.logical_and(s < z, z == n_strip - 1))
        def _():
            rs_send[s] = acc[s].astype(BF16)
            rs_copy(s, 0).start()

        return carry


    def pass_on(i, carry):
        s = nth(i)

        @pl.when(jnp.logical_and(s > z, has_left))
        def _():
            rs_wait(s, 1)
            rs_send[s] = (acc[s] + rs_recv[s].astype(F32)).astype(BF16)
            rs_copy(s, 1).start()

        @pl.when(jnp.logical_and(s < z, has_right))
        def _():
            rs_wait(s, 0)
            rs_send[s] = (acc[s] + rs_recv[s].astype(F32)).astype(BF16)
            rs_copy(s, 0).start()

        return carry

    def sum_step(i, carry):
        cross_strip(i, 0)

        @pl.when(i >= 2)
        def _():
            pass_on(i - 2, 0)

        return carry

    lax.fori_loop(0, n_strip, sum_step, 0)
    lax.fori_loop(n_strip - 2, n_strip - 1, pass_on, 0)

    @pl.when(has_left)
    def _():
        rs_wait(z, 1)
        acc[z] = acc[z] + rs_recv[z].astype(F32)

    @pl.when(has_right)
    def _():
        rs_wait(n_strip, 0)
        acc[z] = acc[z] + rs_recv[n_strip].astype(F32)

    out[0] = (tokens[0].astype(F32) + acc[z]).astype(BF16)

    def settle(t, carry):
        @pl.when(jnp.logical_and(has_left, t >= z))
        def _():
            n_copy(t, 0).wait_send()

        @pl.when(jnp.logical_and(has_right, t <= z))
        def _():
            n_copy(t, 1).wait_send()

        for o, p in enumerate(peers):
            kv_copy(v, t, p, kv_send.at[o, t]).wait_send()
            kv_copy(p, t, mate, fwd_send.at[o, t]).wait_send()
            if relay:
                kv_copy(p, t, mate, rel_send.at[o, t], o).wait_send()
        if relay:
            kv_copy(far, t, mate, fwd_send.at[2, t]).wait_send()
        kv_copy(v, t, mate, kv_send.at[n_chip - 1, t]).wait_send()

        @pl.when(t > z)
        def _():
            rs_copy(t, 1).wait_send()

        @pl.when(t < z)
        def _():
            rs_copy(t, 0).wait_send()

        return carry

    lax.fori_loop(0, n_strip, settle, 0)


def per_device(n_view, n_strip, tokens, source_ids, source_count, *weights):
    rows, width = tokens.shape[1:]
    hc = weights[0].shape[1]
    hidden = weights[-2].shape[1]
    slots = source_ids.shape[2]
    up = next(u for u in (384, 256, 128, hidden) if hidden % u == 0)
    n_up = hidden // up
    n_chip = n_view // 2
    dma = pltpu.SemaphoreType.DMA
    vmem = pl.BlockSpec(memory_space=pltpu.VMEM)
    hbm = pl.BlockSpec(memory_space=pl.ANY)
    return pl.pallas_call(
        functools.partial(kernel, n_view, n_strip, slots),
        out_shape=jax.ShapeDtypeStruct(tokens.shape, tokens.dtype),
        in_specs=[hbm, hbm, vmem] + [hbm] * len(weights),
        out_specs=vmem,
        scratch_shapes=[
            pltpu.SMEM(source_ids.shape[::-1], jnp.int32),
            pltpu.SMEM(source_count.shape[::-1], jnp.int32),
            pltpu.VMEM((6, width, hc), BF16),
            pltpu.VMEM((2, hc, width), BF16),
            pltpu.VMEM((n_up, width, up), BF16),
            pltpu.VMEM((n_up, up, width), BF16),
            pltpu.VMEM((n_strip, rows, width), BF16),
            pltpu.VMEM((4, n_strip, rows, hc), BF16),
            pltpu.VMEM((n_view * n_strip, rows, 2 * hc), BF16),
            pltpu.VMEM((slots, rows, 2 * hc), BF16),
            pltpu.VMEM((n_strip, rows, width), F32),
            pltpu.VMEM((n_strip, rows, width), BF16),
            pltpu.VMEM((n_strip + 1, rows, width), BF16),
            dma((10 + 2 * n_up,)),
            dma((2, n_strip)),
            dma((n_strip,)),
            dma((n_chip, n_strip)),
            dma((n_chip, n_strip)),
            dma((2, n_strip)),
            dma((n_view * n_strip, 2)),
            dma((n_strip,)),
            dma((n_strip + 1,)),
        ],
        compiler_params=pltpu.CompilerParams(
            collective_id=0, has_side_effects=True, vmem_limit_bytes=60 * 1024 * 1024
        ),
    )(source_ids.transpose(2, 1, 0), source_count.T, tokens, *weights)


def solution(mesh):
    column, row = P(None, "strip"), P("strip", None)
    in_specs = (
        P("view", "strip", None),
        P(),
        P(),
        column,
        column,
        column,
        row,
        column,
        column,
        column,
        row,
        column,
        row,
    )
    return jax.shard_map(
        functools.partial(per_device, mesh.shape["view"], mesh.shape["strip"]),
        mesh=mesh,
        in_specs=in_specs,
        out_specs=P("view", "strip", None),
        check_vma=False,
    )
```

```python
import functools
import math

import jax
import jax.numpy as jnp
from jax import lax
from jax.experimental import pallas as pl
from jax.experimental.pallas import tpu as pltpu
from jax.sharding import PartitionSpec as P

HEAD_DIM = 64
LANES = 128
MESH = pl.DeviceIdType.MESH
F32 = jnp.float32
BF16 = jnp.bfloat16


def dot(a, b):
    return jnp.dot(a, b, preferred_element_type=F32)


def dot_nt(a, b):
    return lax.dot_general(a, b, (((1,), (1,)), ((), ())), preferred_element_type=F32)


def attend(q, keys, values, bias):
    cols = q.shape[1]
    parts = []
    for lo in range(0, cols, LANES):
        hi = min(lo + LANES, cols)
        q_block = q[:, lo:hi] * jnp.asarray(1.0 / math.sqrt(HEAD_DIM), BF16)
        k_block, v_block = keys(lo, hi), values(lo, hi)
        lane = lax.broadcasted_iota(jnp.int32, q_block.shape, 1)
        result = None
        for head in range((hi - lo) // HEAD_DIM):
            inside = jnp.logical_and(lane >= head * HEAD_DIM, lane < (head + 1) * HEAD_DIM)
            scores = dot_nt(jnp.where(inside, q_block, jnp.zeros_like(q_block)), k_block)
            if bias is not None:
                scores = scores + bias
            top = jnp.max(scores, axis=-1, keepdims=True)
            weights = jnp.exp(scores - top)
            total = jnp.sum(weights, axis=-1, keepdims=True)
            mixed = dot(weights.astype(BF16), v_block) * (1.0 / total)
            result = mixed if result is None else jnp.where(inside, mixed, result)
        parts.append(result.astype(BF16))
    return parts[0] if len(parts) == 1 else jnp.concatenate(parts, axis=1)


def kernel(
    n_view,
    n_strip,
    slots,
    ids_in,
    counts_in,
    tokens,
    w_sq,
    w_sk,
    w_sv,
    w_so,
    w_cq,
    w_ck,
    w_cv,
    w_co,
    w_up,
    w_down,
    out,
    ids,
    counts,
    wa,
    wo,
    wm,
    md,
    nbuf,
    proj,
    kv,
    kbuf,
    acc,
    rs_send,
    rs_recv,
    w_sem,
    n_send,
    n_recv,
    kv_send,
    fwd_send,
    kv_recv,
    rs_ssem,
    rs_rsem,
):
    v = lax.axis_index("view")
    z = lax.axis_index("strip")
    n_chip = n_view // 2
    chip, core = v // 2, v % 2
    mate = chip * 2 + 1 - core
    rows = tokens.shape[1]
    hc = w_sq.shape[1]
    n_up, _, up = wm.shape
    pair = wa.shape[2] // hc
    has_left, has_right = z > 0, z < n_strip - 1

    loads = []

    def load(src, dst):
        copy = pltpu.make_async_copy(src, dst, w_sem.at[len(loads)])
        copy.start()
        loads.append(copy)

    def load_columns(src, i):
        if pair == 2:
            load(src, wa.at[i // 2, :, pl.ds(i % 2 * hc, hc)])
        else:
            load(src, wa.at[i])

    load_columns(w_ck, 4)
    load_columns(w_cv, 5)

    barrier = pltpu.get_barrier_semaphore()

    def greet(view, strip):
        pl.semaphore_signal(barrier, inc=1, device_id=(view, strip), device_id_type=MESH)

    peers = [lax.rem(chip + o, n_chip) * 2 + core for o in range(1, n_chip)]
    for p in peers:
        greet(p, z)
    greet(mate, z)

    @pl.when(has_left)
    def _():
        greet(v, z - 1)

    @pl.when(has_right)
    def _():
        greet(v, z + 1)

    wide = tokens[0].astype(F32)
    nbuf[z] = (wide * lax.rsqrt(jnp.mean(wide * wide, axis=-1, keepdims=True) + 1e-06)).astype(BF16)
    pl.semaphore_wait(
        barrier, len(peers) + 1 + jnp.where(has_left, 1, 0) + jnp.where(has_right, 1, 0)
    )

    def n_copy(b, side):
        return pltpu.make_async_remote_copy(
            src_ref=nbuf.at[b],
            dst_ref=nbuf.at[b],
            send_sem=n_send.at[side, b],
            recv_sem=n_recv.at[b],
            device_id=(v, z + (2 * side - 1)),
            device_id_type=MESH,
        )

    def kv_copy(view, t, to, sem):
        index = view * n_strip + t
        return pltpu.make_async_remote_copy(
            src_ref=kv.at[index],
            dst_ref=kv.at[index],
            send_sem=sem,
            recv_sem=kv_recv.at[index],
            device_id=(to, z),
            device_id_type=MESH,
        )

    def share(t):
        for o, p in enumerate(peers):
            kv_copy(v, t, p, kv_send.at[o, t]).start()
        kv_copy(v, t, mate, kv_send.at[n_chip - 1, t]).start()

    def forward(t):
        for o, p in enumerate(peers):
            kv_copy(p, t, mate, fwd_send.at[o, t]).wait_recv()
            kv_copy(p, t, mate, fwd_send.at[o, t]).start()

    def project_kv(b):
        x = nbuf[b]
        index = v * n_strip + b
        if pair == 2:
            kv[index] = dot(x, wa[2]).astype(BF16)
        else:
            kv[index, :, 0:hc] = dot(x, wa[4]).astype(BF16)
            kv[index, :, hc : 2 * hc] = dot(x, wa[5]).astype(BF16)
        share(b)

    def project_qkv(b):
        def one(i, carry):
            product = dot(nbuf[b], wa[i]).astype(BF16)
            for half in range(pair):
                proj[pair * i + half, b] = product[:, half * hc : (half + 1) * hc]
            return carry

        lax.fori_loop(0, 4 // pair, one, 0)

    def project_mlp(b):
        def mlp(j, carry):
            hidden = jax.nn.gelu(dot(nbuf[b], wm[j])).astype(BF16)
            term = dot(hidden, md[j])

            @pl.when(j == 0)
            def _():
                acc[b] = term

            @pl.when(j > 0)
            def _():
                acc[b] = acc[b] + term

            return carry

        lax.fori_loop(0, n_up, mlp, 0)

    def at_distance(d, fn):
        @pl.when(z - d >= 0)
        def _():
            fn(z - d)

        @pl.when(jnp.logical_and(z + d < n_strip, d > 0))
        def _():
            fn(z + d)

    @pl.when(has_left)
    def _():
        n_copy(z, 0).start()

    @pl.when(has_right)
    def _():
        n_copy(z, 1).start()

    load_columns(w_sq, 0)
    load_columns(w_sk, 1)
    load_columns(w_sv, 2)
    load_columns(w_cq, 3)
    for j in range(n_up):
        load(w_up.at[:, pl.ds(j * up, up)], wm.at[j])
    for j in range(n_up):
        load(w_down.at[pl.ds(j * up, up)], md.at[j])
    load(w_so, wo.at[pl.ds(0, hc)])
    load(w_co, wo.at[pl.ds(hc, hc)])
    load(ids_in, ids)
    load(counts_in, counts)

    for copy in loads[:2]:
        copy.wait()
    project_kv(z)
    for copy in loads[2:]:
        copy.wait()
    project_qkv(z)

    def gather_step(d, carry):
        @pl.when(z - d >= 0)
        def _():
            n_copy(z - d, 1).wait_recv()

            @pl.when(has_right)
            def _():
                n_copy(z - d, 1).start()

        @pl.when(z + d < n_strip)
        def _():
            n_copy(z + d, 0).wait_recv()

            @pl.when(has_left)
            def _():
                n_copy(z + d, 0).start()

        def both(fn):
            def one(side, c):
                b = z + (2 * side - 1) * d

                @pl.when(jnp.logical_and(b >= 0, b < n_strip))
                def _():
                    fn(b)

                return c

            lax.fori_loop(0, 2, one, 0)

        both(project_kv)
        both(project_qkv)

        def mlp_at(before, c):
            e = d - before

            @pl.when(jnp.logical_and(before == 0, z - d >= 0))
            def _():
                project_mlp(z - d)

            right_now = jnp.logical_and(before == 0, z - d < 0)
            right_late = jnp.logical_and(before == 1, z - e >= 0)
            due = jnp.logical_and(jnp.logical_or(right_now, right_late), e > 0)

            @pl.when(jnp.logical_and(due, z + e < n_strip))
            def _():
                project_mlp(z + e)

            return c

        lax.fori_loop(0, 2, mlp_at, 0)
        at_distance(d - 1, forward)
        return carry

    lax.fori_loop(1, n_strip, gather_step, 0)

    def nth(i):
        low = n_strip - 1 - i
        low = jnp.where(low > z, low, low - 1)
        high = jnp.where(i < z, i, i + 1)
        return jnp.where(i == n_strip - 1, z, jnp.where(z < n_strip // 2, low, high))

    def self_strip(i, carry):
        s = nth(i)

        def columns(i):
            return lambda lo, hi: proj[i, :, :, lo:hi].reshape(n_strip * rows, hi - lo)

        proj[0, s] = attend(proj[0, s], columns(1), columns(2), None)
        return carry

    lax.fori_loop(0, n_strip - 2, self_strip, 0)
    at_distance(n_strip - 1, forward)
    lax.fori_loop(n_strip - 2, n_strip - 1, self_strip, 0)

    def from_mate(t, carry):
        kv_copy(mate, t, mate, fwd_send.at[0, t]).wait_recv()
        for p in peers:
            kv_copy(p + 1 - 2 * core, t, mate, fwd_send.at[0, t]).wait_recv()
        return carry

    lax.fori_loop(0, n_strip, from_mate, 0)

    def rs_copy(s, side):
        slot = jnp.where(jnp.logical_and(side == 0, s == z - 1), n_strip, s)
        return pltpu.make_async_remote_copy(
            src_ref=rs_send.at[s],
            dst_ref=rs_recv.at[slot],
            send_sem=rs_ssem.at[s],
            recv_sem=rs_rsem.at[slot],
            device_id=(v, z + (2 * side - 1)),
            device_id_type=MESH,
        )

    def rs_wait(slot, side):
        pltpu.make_async_remote_copy(
            src_ref=rs_send.at[0],
            dst_ref=rs_recv.at[slot],
            send_sem=rs_ssem.at[0],
            recv_sem=rs_rsem.at[slot],
            device_id=(v, z + (2 * side - 1)),
            device_id_type=MESH,
        ).wait_recv()

    def cross_strip(i, carry):
        s = nth(i)
        for k in range(slots):
            kbuf[k] = kv[ids[k, s, v]]
        count = counts[s, v]
        column = lax.broadcasted_iota(jnp.int32, (1, slots * rows), 1)
        bias = jnp.where(column < count * rows, 0.0, -1e30).astype(F32)

        def columns(start):
            return lambda lo, hi: kbuf[:, :, start + lo : start + hi].reshape(slots * rows, hi - lo)

        mixed = attend(proj[3, s], columns(0), columns(hc), bias)
        acc[s] = acc[s] + dot(jnp.concatenate([proj[0, s], mixed], axis=1), wo[...])

        @pl.when(jnp.logical_and(s > z, z == 0))
        def _():
            rs_send[s] = acc[s].astype(BF16)
            rs_copy(s, 1).start()

        @pl.when(jnp.logical_and(s < z, z == n_strip - 1))
        def _():
            rs_send[s] = acc[s].astype(BF16)
            rs_copy(s, 0).start()

        return carry


    def pass_on(i, carry):
        s = nth(i)

        @pl.when(jnp.logical_and(s > z, has_left))
        def _():
            rs_wait(s, 1)
            rs_send[s] = (acc[s] + rs_recv[s].astype(F32)).astype(BF16)
            rs_copy(s, 1).start()

        @pl.when(jnp.logical_and(s < z, has_right))
        def _():
            rs_wait(s, 0)
            rs_send[s] = (acc[s] + rs_recv[s].astype(F32)).astype(BF16)
            rs_copy(s, 0).start()

        return carry

    lax.fori_loop(0, n_strip - 1, cross_strip, 0)

    last = n_strip - 1
    self_strip(last, 0)
    lax.fori_loop(0, min(1, last), pass_on, 0)
    project_mlp(z)
    lax.fori_loop(1, min(2, last), pass_on, 0)
    cross_strip(last, 0)
    lax.fori_loop(2, max(2, last), pass_on, 0)

    @pl.when(has_left)
    def _():
        rs_wait(z, 1)
        acc[z] = acc[z] + rs_recv[z].astype(F32)

    @pl.when(has_right)
    def _():
        rs_wait(n_strip, 0)
        acc[z] = acc[z] + rs_recv[n_strip].astype(F32)

    out[0] = (tokens[0].astype(F32) + acc[z]).astype(BF16)

    def settle(t, carry):
        @pl.when(jnp.logical_and(has_left, t >= z))
        def _():
            n_copy(t, 0).wait_send()

        @pl.when(jnp.logical_and(has_right, t <= z))
        def _():
            n_copy(t, 1).wait_send()

        for o, p in enumerate(peers):
            kv_copy(v, t, p, kv_send.at[o, t]).wait_send()
            kv_copy(p, t, mate, fwd_send.at[o, t]).wait_send()
        kv_copy(v, t, mate, kv_send.at[n_chip - 1, t]).wait_send()

        @pl.when(t > z)
        def _():
            rs_copy(t, 1).wait_send()

        @pl.when(t < z)
        def _():
            rs_copy(t, 0).wait_send()

        return carry

    lax.fori_loop(0, n_strip, settle, 0)


def per_device(n_view, n_strip, tokens, source_ids, source_count, *weights):
    rows, width = tokens.shape[1:]
    hc = weights[0].shape[1]
    hidden = weights[-2].shape[1]
    slots = source_ids.shape[2]
    up = next(u for u in (768, 512, 256, 128, hidden) if hidden % u == 0)
    n_up = hidden // up
    pair = 2 if hc % LANES == 0 else 1
    n_chip = n_view // 2
    dma = pltpu.SemaphoreType.DMA
    vmem = pl.BlockSpec(memory_space=pltpu.VMEM)
    hbm = pl.BlockSpec(memory_space=pl.ANY)
    return pl.pallas_call(
        functools.partial(kernel, n_view, n_strip, slots),
        out_shape=jax.ShapeDtypeStruct(tokens.shape, tokens.dtype),
        in_specs=[hbm, hbm, vmem] + [hbm] * len(weights),
        out_specs=vmem,
        scratch_shapes=[
            pltpu.SMEM(source_ids.shape[::-1], jnp.int32),
            pltpu.SMEM(source_count.shape[::-1], jnp.int32),
            pltpu.VMEM((6 // pair, width, pair * hc), BF16),
            pltpu.VMEM((2 * hc, width), BF16),
            pltpu.VMEM((n_up, width, up), BF16),
            pltpu.VMEM((n_up, up, width), BF16),
            pltpu.VMEM((n_strip, rows, width), BF16),
            pltpu.VMEM((4, n_strip, rows, hc), BF16),
            pltpu.VMEM((n_view * n_strip, rows, 2 * hc), BF16),
            pltpu.VMEM((slots, rows, 2 * hc), BF16),
            pltpu.VMEM((n_strip, rows, width), F32),
            pltpu.VMEM((n_strip, rows, width), BF16),
            pltpu.VMEM((n_strip + 1, rows, width), BF16),
            dma((10 + 2 * n_up,)),
            dma((2, n_strip)),
            dma((n_strip,)),
            dma((n_chip, n_strip)),
            dma((n_chip, n_strip)),
            dma((n_view * n_strip,)),
            dma((n_strip,)),
            dma((n_strip + 1,)),
        ],
        compiler_params=pltpu.CompilerParams(
            collective_id=0, has_side_effects=True, vmem_limit_bytes=60 * 1024 * 1024
        ),
    )(source_ids.transpose(2, 1, 0), source_count.T, tokens, *weights)


def solution(mesh):
    column, row = P(None, "strip"), P("strip", None)
    in_specs = (
        P("view", "strip", None),
        P(),
        P(),
        column,
        column,
        column,
        row,
        column,
        column,
        column,
        row,
        column,
        row,
    )
    return jax.shard_map(
        functools.partial(per_device, mesh.shape["view"], mesh.shape["strip"]),
        mesh=mesh,
        in_specs=in_specs,
        out_specs=P("view", "strip", None),
        check_vma=False,
    )
```

```python
import functools
import math

import jax
import jax.numpy as jnp
from jax import lax
from jax.experimental import pallas as pl
from jax.experimental.pallas import tpu as pltpu
from jax.sharding import PartitionSpec as P

HEAD_DIM = 64
LANES = 128
MESH = pl.DeviceIdType.MESH
F32 = jnp.float32
BF16 = jnp.bfloat16


def dot(a, b):
    return jnp.dot(a, b, preferred_element_type=F32)


def dot_nt(a, b):
    return lax.dot_general(a, b, (((1,), (1,)), ((), ())), preferred_element_type=F32)


def attend(q, keys, values, bias):
    cols = q.shape[1]
    parts = []
    for lo in range(0, cols, LANES):
        hi = min(lo + LANES, cols)
        q_block = q[:, lo:hi] * jnp.asarray(1.0 / math.sqrt(HEAD_DIM), BF16)
        k_block, v_block = keys(lo, hi), values(lo, hi)
        lane = lax.broadcasted_iota(jnp.int32, q_block.shape, 1)
        heads = (hi - lo) // HEAD_DIM
        inside = [
            jnp.logical_and(lane >= h * HEAD_DIM, lane < (h + 1) * HEAD_DIM) for h in range(heads)
        ]
        stacked = jnp.concatenate([jnp.where(m, q_block, jnp.zeros_like(q_block)) for m in inside])
        scores = dot_nt(stacked, k_block)
        if bias is not None:
            scores = scores + bias
        top = jnp.max(scores, axis=-1, keepdims=True)
        weights = jnp.exp(scores - top)
        total = jnp.sum(weights, axis=-1, keepdims=True)
        mixed = dot(weights.astype(BF16), v_block) * (1.0 / total)
        count = q.shape[0]
        result = mixed[:count]
        for h in range(1, heads):
            result = jnp.where(inside[h], mixed[h * count : (h + 1) * count], result)
        parts.append(result.astype(BF16))
    return parts[0] if len(parts) == 1 else jnp.concatenate(parts, axis=1)


def kernel(
    n_view,
    n_strip,
    slots,
    ids_in,
    counts_in,
    tokens,
    w_sq,
    w_sk,
    w_sv,
    w_so,
    w_cq,
    w_ck,
    w_cv,
    w_co,
    w_up,
    w_down,
    out,
    ids,
    counts,
    wa,
    wo,
    wm,
    md,
    nbuf,
    proj,
    kv,
    kbuf,
    acc,
    rs_send,
    rs_recv,
    w_sem,
    n_send,
    n_recv,
    kv_send,
    fwd_send,
    kv_recv,
    rs_ssem,
    rs_rsem,
):
    v = lax.axis_index("view")
    z = lax.axis_index("strip")
    n_chip = n_view // 2
    chip, core = v // 2, v % 2
    mate = chip * 2 + 1 - core
    rows = tokens.shape[1]
    hc = w_sq.shape[1]
    n_up, _, up = wm.shape
    pair = wa.shape[2] // hc
    has_left, has_right = z > 0, z < n_strip - 1

    loads = []

    def load(src, dst):
        copy = pltpu.make_async_copy(src, dst, w_sem.at[len(loads)])
        copy.start()
        loads.append(copy)

    def load_columns(src, i):
        if pair == 2:
            load(src, wa.at[i // 2, :, pl.ds(i % 2 * hc, hc)])
        else:
            load(src, wa.at[i])

    load_columns(w_ck, 4)
    load_columns(w_cv, 5)

    barrier = pltpu.get_barrier_semaphore()

    def greet(view, strip):
        pl.semaphore_signal(barrier, inc=1, device_id=(view, strip), device_id_type=MESH)

    peers = [lax.rem(chip + o, n_chip) * 2 + core for o in range(1, n_chip)]
    for p in peers:
        greet(p, z)
    greet(mate, z)

    @pl.when(has_left)
    def _():
        greet(v, z - 1)

    @pl.when(has_right)
    def _():
        greet(v, z + 1)

    wide = tokens[0].astype(F32)
    nbuf[z] = (wide * lax.rsqrt(jnp.mean(wide * wide, axis=-1, keepdims=True) + 1e-06)).astype(BF16)
    pl.semaphore_wait(
        barrier, len(peers) + 1 + jnp.where(has_left, 1, 0) + jnp.where(has_right, 1, 0)
    )

    def n_copy(b, side):
        return pltpu.make_async_remote_copy(
            src_ref=nbuf.at[b],
            dst_ref=nbuf.at[b],
            send_sem=n_send.at[side, b],
            recv_sem=n_recv.at[b],
            device_id=(v, z + (2 * side - 1)),
            device_id_type=MESH,
        )

    def kv_copy(view, t, to, sem):
        index = view * n_strip + t
        return pltpu.make_async_remote_copy(
            src_ref=kv.at[index],
            dst_ref=kv.at[index],
            send_sem=sem,
            recv_sem=kv_recv.at[index],
            device_id=(to, z),
            device_id_type=MESH,
        )

    def share(t):
        for o, p in enumerate(peers):
            kv_copy(v, t, p, kv_send.at[o, t]).start()
        kv_copy(v, t, mate, kv_send.at[n_chip - 1, t]).start()

    def forward(t):
        for o, p in enumerate(peers):
            kv_copy(p, t, mate, fwd_send.at[o, t]).wait_recv()
            kv_copy(p, t, mate, fwd_send.at[o, t]).start()

    def project_kv(b):
        x = nbuf[b]
        index = v * n_strip + b
        if pair == 2:
            kv[index] = dot(x, wa[2]).astype(BF16)
        else:
            kv[index, :, 0:hc] = dot(x, wa[4]).astype(BF16)
            kv[index, :, hc : 2 * hc] = dot(x, wa[5]).astype(BF16)
        share(b)

    def project_qkv(b):
        def one(i, carry):
            product = dot(nbuf[b], wa[i]).astype(BF16)
            for half in range(pair):
                proj[pair * i + half, b] = product[:, half * hc : (half + 1) * hc]
            return carry

        lax.fori_loop(0, 4 // pair, one, 0)

    def project_mlp(b):
        def mlp(j, carry):
            hidden = jax.nn.gelu(dot(nbuf[b], wm[j])).astype(BF16)
            term = dot(hidden, md[j])

            @pl.when(j == 0)
            def _():
                acc[b] = term

            @pl.when(j > 0)
            def _():
                acc[b] = acc[b] + term

            return carry

        lax.fori_loop(0, n_up, mlp, 0)

    def at_distance(d, fn):
        @pl.when(z - d >= 0)
        def _():
            fn(z - d)

        @pl.when(jnp.logical_and(z + d < n_strip, d > 0))
        def _():
            fn(z + d)

    @pl.when(has_left)
    def _():
        n_copy(z, 0).start()

    @pl.when(has_right)
    def _():
        n_copy(z, 1).start()

    load_columns(w_sq, 0)
    load_columns(w_sk, 1)
    load_columns(w_sv, 2)
    load_columns(w_cq, 3)
    for j in range(n_up):
        load(w_up.at[:, pl.ds(j * up, up)], wm.at[j])
    for j in range(n_up):
        load(w_down.at[pl.ds(j * up, up)], md.at[j])
    load(w_so, wo.at[pl.ds(0, hc)])
    load(w_co, wo.at[pl.ds(hc, hc)])
    load(ids_in, ids)
    load(counts_in, counts)

    for copy in loads[:2]:
        copy.wait()
    project_kv(z)
    for copy in loads[2:]:
        copy.wait()
    project_qkv(z)

    def gather_step(d, carry):
        @pl.when(z - d >= 0)
        def _():
            n_copy(z - d, 1).wait_recv()

            @pl.when(has_right)
            def _():
                n_copy(z - d, 1).start()

        @pl.when(z + d < n_strip)
        def _():
            n_copy(z + d, 0).wait_recv()

            @pl.when(has_left)
            def _():
                n_copy(z + d, 0).start()

        def both(fn):
            def one(side, c):
                b = z + (2 * side - 1) * d

                @pl.when(jnp.logical_and(b >= 0, b < n_strip))
                def _():
                    fn(b)

                return c

            lax.fori_loop(0, 2, one, 0)

        both(project_kv)
        both(project_qkv)

        def mlp_at(before, c):
            e = d - before

            @pl.when(jnp.logical_and(before == 0, z - d >= 0))
            def _():
                project_mlp(z - d)

            right_now = jnp.logical_and(before == 0, z - d < 0)
            right_late = jnp.logical_and(before == 1, z - e >= 0)
            due = jnp.logical_and(jnp.logical_or(right_now, right_late), e > 0)

            @pl.when(jnp.logical_and(due, z + e < n_strip))
            def _():
                project_mlp(z + e)

            return c

        lax.fori_loop(0, 2, mlp_at, 0)
        at_distance(d - 1, forward)
        return carry

    lax.fori_loop(1, n_strip, gather_step, 0)

    def nth(i):
        low = n_strip - 1 - i
        low = jnp.where(low > z, low, low - 1)
        high = jnp.where(i < z, i, i + 1)
        return jnp.where(i == n_strip - 1, z, jnp.where(z < n_strip // 2, low, high))

    def self_strip(i, carry):
        s = nth(i)

        def columns(i):
            return lambda lo, hi: proj[i, :, :, lo:hi].reshape(n_strip * rows, hi - lo)

        proj[0, s] = attend(proj[0, s], columns(1), columns(2), None)
        return carry

    def self_first(i, carry):
        self_strip(i, 0)

        @pl.when(i == 0)
        def _():
            at_distance(n_strip - 1, forward)

        return carry

    lax.fori_loop(0, 2, self_first, 0)

    def from_mate(t, carry):
        kv_copy(mate, t, mate, fwd_send.at[0, t]).wait_recv()
        for p in peers:
            kv_copy(p + 1 - 2 * core, t, mate, fwd_send.at[0, t]).wait_recv()
        return carry

    lax.fori_loop(0, n_strip, from_mate, 0)

    def rs_copy(s, side):
        slot = jnp.where(jnp.logical_and(side == 0, s == z - 1), n_strip, s)
        return pltpu.make_async_remote_copy(
            src_ref=rs_send.at[s],
            dst_ref=rs_recv.at[slot],
            send_sem=rs_ssem.at[s],
            recv_sem=rs_rsem.at[slot],
            device_id=(v, z + (2 * side - 1)),
            device_id_type=MESH,
        )

    def rs_wait(slot, side):
        pltpu.make_async_remote_copy(
            src_ref=rs_send.at[0],
            dst_ref=rs_recv.at[slot],
            send_sem=rs_ssem.at[0],
            recv_sem=rs_rsem.at[slot],
            device_id=(v, z + (2 * side - 1)),
            device_id_type=MESH,
        ).wait_recv()

    def cross_strip(i, carry):
        s = nth(i)
        for k in range(slots):
            kbuf[k] = kv[ids[k, s, v]]
        count = counts[s, v]
        column = lax.broadcasted_iota(jnp.int32, (1, slots * rows), 1)
        bias = jnp.where(column < count * rows, 0.0, -1e30).astype(F32)

        def columns(start):
            return lambda lo, hi: kbuf[:, :, start + lo : start + hi].reshape(slots * rows, hi - lo)

        mixed = attend(proj[3, s], columns(0), columns(hc), bias)
        acc[s] = acc[s] + dot(jnp.concatenate([proj[0, s], mixed], axis=1), wo[...])

        @pl.when(jnp.logical_and(s > z, z == 0))
        def _():
            rs_send[s] = acc[s].astype(BF16)
            rs_copy(s, 1).start()

        @pl.when(jnp.logical_and(s < z, z == n_strip - 1))
        def _():
            rs_send[s] = acc[s].astype(BF16)
            rs_copy(s, 0).start()

        return carry


    def pass_on(i, carry):
        s = nth(i)

        @pl.when(jnp.logical_and(s > z, has_left))
        def _():
            rs_wait(s, 1)
            rs_send[s] = (acc[s] + rs_recv[s].astype(F32)).astype(BF16)
            rs_copy(s, 1).start()

        @pl.when(jnp.logical_and(s < z, has_right))
        def _():
            rs_wait(s, 0)
            rs_send[s] = (acc[s] + rs_recv[s].astype(F32)).astype(BF16)
            rs_copy(s, 0).start()

        return carry

    last = n_strip - 1

    def sum_step(i, carry):
        @pl.when(i == last)
        def _():
            pass_on(0, 0)
            project_mlp(z)
            lax.fori_loop(1, min(2, last), pass_on, 0)

        cross_strip(i, 0)

        @pl.when(i + 2 < n_strip)
        def _():
            self_strip(i + 2, 0)

        return carry

    lax.fori_loop(0, n_strip, sum_step, 0)
    lax.fori_loop(min(2, last), last, pass_on, 0)

    @pl.when(has_left)
    def _():
        rs_wait(z, 1)
        acc[z] = acc[z] + rs_recv[z].astype(F32)

    @pl.when(has_right)
    def _():
        rs_wait(n_strip, 0)
        acc[z] = acc[z] + rs_recv[n_strip].astype(F32)

    out[0] = (tokens[0].astype(F32) + acc[z]).astype(BF16)

    def settle(t, carry):
        @pl.when(jnp.logical_and(has_left, t >= z))
        def _():
            n_copy(t, 0).wait_send()

        @pl.when(jnp.logical_and(has_right, t <= z))
        def _():
            n_copy(t, 1).wait_send()

        for o, p in enumerate(peers):
            kv_copy(v, t, p, kv_send.at[o, t]).wait_send()
            kv_copy(p, t, mate, fwd_send.at[o, t]).wait_send()
        kv_copy(v, t, mate, kv_send.at[n_chip - 1, t]).wait_send()

        @pl.when(t > z)
        def _():
            rs_copy(t, 1).wait_send()

        @pl.when(t < z)
        def _():
            rs_copy(t, 0).wait_send()

        return carry

    lax.fori_loop(0, n_strip, settle, 0)


def per_device(n_view, n_strip, tokens, source_ids, source_count, *weights):
    rows, width = tokens.shape[1:]
    hc = weights[0].shape[1]
    hidden = weights[-2].shape[1]
    slots = source_ids.shape[2]
    up = next(u for u in (768, 512, 256, 128, hidden) if hidden % u == 0)
    n_up = hidden // up
    pair = 2 if hc % LANES == 0 else 1
    n_chip = n_view // 2
    dma = pltpu.SemaphoreType.DMA
    vmem = pl.BlockSpec(memory_space=pltpu.VMEM)
    hbm = pl.BlockSpec(memory_space=pl.ANY)
    return pl.pallas_call(
        functools.partial(kernel, n_view, n_strip, slots),
        out_shape=jax.ShapeDtypeStruct(tokens.shape, tokens.dtype),
        in_specs=[hbm, hbm, vmem] + [hbm] * len(weights),
        out_specs=vmem,
        scratch_shapes=[
            pltpu.SMEM(source_ids.shape[::-1], jnp.int32),
            pltpu.SMEM(source_count.shape[::-1], jnp.int32),
            pltpu.VMEM((6 // pair, width, pair * hc), BF16),
            pltpu.VMEM((2 * hc, width), BF16),
            pltpu.VMEM((n_up, width, up), BF16),
            pltpu.VMEM((n_up, up, width), BF16),
            pltpu.VMEM((n_strip, rows, width), BF16),
            pltpu.VMEM((4, n_strip, rows, hc), BF16),
            pltpu.VMEM((n_view * n_strip, rows, 2 * hc), BF16),
            pltpu.VMEM((slots, rows, 2 * hc), BF16),
            pltpu.VMEM((n_strip, rows, width), F32),
            pltpu.VMEM((n_strip, rows, width), BF16),
            pltpu.VMEM((n_strip + 1, rows, width), BF16),
            dma((10 + 2 * n_up,)),
            dma((2, n_strip)),
            dma((n_strip,)),
            dma((n_chip, n_strip)),
            dma((n_chip, n_strip)),
            dma((n_view * n_strip,)),
            dma((n_strip,)),
            dma((n_strip + 1,)),
        ],
        compiler_params=pltpu.CompilerParams(
            collective_id=0, has_side_effects=True, vmem_limit_bytes=60 * 1024 * 1024
        ),
    )(source_ids.transpose(2, 1, 0), source_count.T, tokens, *weights)


def solution(mesh):
    column, row = P(None, "strip"), P("strip", None)
    in_specs = (
        P("view", "strip", None),
        P(),
        P(),
        column,
        column,
        column,
        row,
        column,
        column,
        column,
        row,
        column,
        row,
    )
    return jax.shard_map(
        functools.partial(per_device, mesh.shape["view"], mesh.shape["strip"]),
        mesh=mesh,
        in_specs=in_specs,
        out_specs=P("view", "strip", None),
        check_vma=False,
    )
```

```python
import functools
import math

import jax
import jax.numpy as jnp
from jax import lax
from jax.experimental import pallas as pl
from jax.experimental.pallas import tpu as pltpu
from jax.sharding import PartitionSpec as P

HEAD_DIM = 64
LANES = 128
PARTS = 2
MESH = pl.DeviceIdType.MESH
F32 = jnp.float32
BF16 = jnp.bfloat16


def dot(a, b):
    return jnp.dot(a, b, preferred_element_type=F32)


def dot_nt(a, b):
    return lax.dot_general(a, b, (((1,), (1,)), ((), ())), preferred_element_type=F32)


def attend(q, keys, values, bias):
    cols = q.shape[1]
    parts = []
    for lo in range(0, cols, LANES):
        hi = min(lo + LANES, cols)
        q_block = q[:, lo:hi] * jnp.asarray(1.0 / math.sqrt(HEAD_DIM), BF16)
        k_block, v_block = keys(lo, hi), values(lo, hi)
        lane = lax.broadcasted_iota(jnp.int32, q_block.shape, 1)
        heads = (hi - lo) // HEAD_DIM
        inside = [
            jnp.logical_and(lane >= h * HEAD_DIM, lane < (h + 1) * HEAD_DIM) for h in range(heads)
        ]
        stacked = jnp.concatenate([jnp.where(m, q_block, jnp.zeros_like(q_block)) for m in inside])
        scores = dot_nt(stacked, k_block)
        if bias is not None:
            scores = scores + bias
        top = jnp.max(scores, axis=-1, keepdims=True)
        weights = jnp.exp(scores - top)
        total = jnp.sum(weights, axis=-1, keepdims=True)
        mixed = dot(weights.astype(BF16), v_block) * (1.0 / total)
        count = q.shape[0]
        result = mixed[:count]
        for h in range(1, heads):
            result = jnp.where(inside[h], mixed[h * count : (h + 1) * count], result)
        parts.append(result.astype(BF16))
    return parts[0] if len(parts) == 1 else jnp.concatenate(parts, axis=1)


def kernel(
    n_view,
    n_strip,
    slots,
    ids_in,
    counts_in,
    tokens,
    w_sq,
    w_sk,
    w_sv,
    w_so,
    w_cq,
    w_ck,
    w_cv,
    w_co,
    w_up,
    w_down,
    out,
    ids,
    counts,
    wa,
    wo,
    wm,
    md,
    nbuf,
    proj,
    kv,
    kbuf,
    acc,
    rs_send,
    rs_recv,
    w_sem,
    n_send,
    n_recv,
    kv_send,
    fwd_send,
    kv_recv,
    rs_ssem,
    rs_rsem,
):
    v = lax.axis_index("view")
    z = lax.axis_index("strip")
    n_chip = n_view // 2
    chip, core = v // 2, v % 2
    mate = chip * 2 + 1 - core
    rows = tokens.shape[1]
    hc = w_sq.shape[1]
    part = rows // PARTS
    n_up, _, up = wm.shape
    pair = wa.shape[2] // hc
    has_left, has_right = z > 0, z < n_strip - 1

    loads = []

    def load(src, dst):
        copy = pltpu.make_async_copy(src, dst, w_sem.at[len(loads)])
        copy.start()
        loads.append(copy)

    def load_columns(src, i):
        if pair == 2:
            load(src, wa.at[i // 2, :, pl.ds(i % 2 * hc, hc)])
        else:
            load(src, wa.at[i])

    load_columns(w_ck, 4)
    load_columns(w_cv, 5)

    barrier = pltpu.get_barrier_semaphore()

    def greet(view, strip):
        pl.semaphore_signal(barrier, inc=1, device_id=(view, strip), device_id_type=MESH)

    peers = [lax.rem(chip + o, n_chip) * 2 + core for o in range(1, n_chip)]
    for p in peers:
        greet(p, z)
    greet(mate, z)

    @pl.when(has_left)
    def _():
        greet(v, z - 1)

    @pl.when(has_right)
    def _():
        greet(v, z + 1)

    wide = tokens[0].astype(F32)
    nbuf[z] = (wide * lax.rsqrt(jnp.mean(wide * wide, axis=-1, keepdims=True) + 1e-06)).astype(BF16)
    pl.semaphore_wait(
        barrier, len(peers) + 1 + jnp.where(has_left, 1, 0) + jnp.where(has_right, 1, 0)
    )

    def piece(ref, index, h):
        return ref.at[index, pl.ds(pl.multiple_of(h * part, part), part)]

    def n_copy(b, side, h):
        return pltpu.make_async_remote_copy(
            src_ref=piece(nbuf, b, h),
            dst_ref=piece(nbuf, b, h),
            send_sem=n_send.at[side, b, h],
            recv_sem=n_recv.at[b, h],
            device_id=(v, z + (2 * side - 1)),
            device_id_type=MESH,
        )

    def kv_copy(view, t, h, to, sem):
        index = view * n_strip + t
        return pltpu.make_async_remote_copy(
            src_ref=piece(kv, index, h),
            dst_ref=piece(kv, index, h),
            send_sem=sem,
            recv_sem=kv_recv.at[index, h],
            device_id=(to, z),
            device_id_type=MESH,
        )

    def share(t, h):
        for o, p in enumerate(peers):
            kv_copy(v, t, h, p, kv_send.at[o, t, h]).start()
        kv_copy(v, t, h, mate, kv_send.at[n_chip - 1, t, h]).start()

    def forward(t):
        def one(h, carry):
            for o, p in enumerate(peers):
                kv_copy(p, t, h, mate, fwd_send.at[o, t, h]).wait_recv()
                kv_copy(p, t, h, mate, fwd_send.at[o, t, h]).start()
            return carry

        lax.fori_loop(0, PARTS, one, 0)

    def project_kv(b, h):
        here = pl.ds(pl.multiple_of(h * part, part), part)
        x = nbuf[b, here]
        index = v * n_strip + b
        if pair == 2:
            kv[index, here] = dot(x, wa[2]).astype(BF16)
        else:
            kv[index, here, 0:hc] = dot(x, wa[4]).astype(BF16)
            kv[index, here, hc : 2 * hc] = dot(x, wa[5]).astype(BF16)
        share(b, h)

    def project_qkv(b):
        def one(i, carry):
            product = dot(nbuf[b], wa[i]).astype(BF16)
            for half in range(pair):
                proj[pair * i + half, b] = product[:, half * hc : (half + 1) * hc]
            return carry

        lax.fori_loop(0, 4 // pair, one, 0)

    def project_mlp(b):
        def mlp(j, carry):
            hidden = jax.nn.gelu(dot(nbuf[b], wm[j])).astype(BF16)
            term = dot(hidden, md[j])

            @pl.when(j == 0)
            def _():
                acc[b] = term

            @pl.when(j > 0)
            def _():
                acc[b] = acc[b] + term

            return carry

        lax.fori_loop(0, n_up, mlp, 0)

    def at_distance(d, fn):
        @pl.when(z - d >= 0)
        def _():
            fn(z - d)

        @pl.when(jnp.logical_and(z + d < n_strip, d > 0))
        def _():
            fn(z + d)

    for h in range(PARTS):

        @pl.when(has_left)
        def _():
            n_copy(z, 0, h).start()

        @pl.when(has_right)
        def _():
            n_copy(z, 1, h).start()

    load_columns(w_sq, 0)
    load_columns(w_sk, 1)
    load_columns(w_sv, 2)
    load_columns(w_cq, 3)
    for j in range(n_up):
        load(w_up.at[:, pl.ds(j * up, up)], wm.at[j])
    for j in range(n_up):
        load(w_down.at[pl.ds(j * up, up)], md.at[j])
    load(w_so, wo.at[pl.ds(0, hc)])
    load(w_co, wo.at[pl.ds(hc, hc)])
    load(ids_in, ids)
    load(counts_in, counts)

    for copy in loads[:2]:
        copy.wait()

    def own_kv(h, carry):
        project_kv(z, h)
        return carry

    lax.fori_loop(0, PARTS, own_kv, 0)
    for copy in loads[2:]:
        copy.wait()
    project_qkv(z)

    def gather_step(d, carry):
        def one(fn):
            def side_step(side, c):
                b = z + (2 * side - 1) * d

                @pl.when(jnp.logical_and(b >= 0, b < n_strip))
                def _():
                    fn(b)

                return c

            lax.fori_loop(0, 2, side_step, 0)

        def arrive(h, c):
            @pl.when(z - d >= 0)
            def _():
                n_copy(z - d, 1, h).wait_recv()

                @pl.when(has_right)
                def _():
                    n_copy(z - d, 1, h).start()

            @pl.when(z + d < n_strip)
            def _():
                n_copy(z + d, 0, h).wait_recv()

                @pl.when(has_left)
                def _():
                    n_copy(z + d, 0, h).start()

            one(lambda b: project_kv(b, h))

            late = z + (2 * h - 1) * (d - 1)

            @pl.when((h < 2) & (d > 1) & (late >= 0) & (late < n_strip))
            def _():
                project_mlp(late)

            return c

        lax.fori_loop(0, PARTS, arrive, 0)
        one(project_qkv)
        at_distance(d - 1, forward)
        return carry

    lax.fori_loop(1, n_strip, gather_step, 0)
    at_distance(n_strip - 1, project_mlp)
    at_distance(n_strip - 1, forward)

    def nth(i):
        low = n_strip - 1 - i
        low = jnp.where(low > z, low, low - 1)
        high = jnp.where(i < z, i, i + 1)
        return jnp.where(i == n_strip - 1, z, jnp.where(z < n_strip // 2, low, high))

    def self_strip(i, carry):
        s = nth(i)

        def columns(i):
            return lambda lo, hi: proj[i, :, :, lo:hi].reshape(n_strip * rows, hi - lo)

        proj[0, s] = attend(proj[0, s], columns(1), columns(2), None)
        return carry

    self_strip(0, 0)

    def from_mate(t, carry):
        def one(h, c):
            kv_copy(mate, t, h, mate, fwd_send.at[0, t, h]).wait_recv()
            for p in peers:
                kv_copy(p + 1 - 2 * core, t, h, mate, fwd_send.at[0, t, h]).wait_recv()
            return c

        lax.fori_loop(0, PARTS, one, 0)
        return carry

    lax.fori_loop(0, n_strip, from_mate, 0)

    def rs_copy(s, side, h, slot=None):
        if slot is None:
            slot = jnp.where(jnp.logical_and(side == 0, s == z - 1), n_strip, s)
        return pltpu.make_async_remote_copy(
            src_ref=piece(rs_send, s, h),
            dst_ref=piece(rs_recv, slot, h),
            send_sem=rs_ssem.at[s, h],
            recv_sem=rs_rsem.at[slot, h],
            device_id=(v, z + (2 * side - 1)),
            device_id_type=MESH,
        )

    def send_sum(s, side, h, arrived):
        here = pl.ds(pl.multiple_of(h * part, part), part)
        total = acc[s, here]
        if arrived:
            rs_copy(0, side, h, s).wait_recv()
            total = total + rs_recv[s, here].astype(F32)
        rs_send[s, here] = total.astype(BF16)
        rs_copy(s, side, h).start()

    def cross_strip(i, carry):
        s = nth(i)
        for k in range(slots):
            kbuf[k] = kv[ids[k, s, v]]
        count = counts[s, v]
        column = lax.broadcasted_iota(jnp.int32, (1, slots * rows), 1)
        bias = jnp.where(column < count * rows, 0.0, -1e30).astype(F32)

        def columns(start):
            return lambda lo, hi: kbuf[:, :, start + lo : start + hi].reshape(slots * rows, hi - lo)

        mixed = attend(proj[3, s], columns(0), columns(hc), bias)
        acc[s] = acc[s] + dot(jnp.concatenate([proj[0, s], mixed], axis=1), wo[...])

        def start(h, c):
            @pl.when(jnp.logical_and(s > z, z == 0))
            def _():
                send_sum(s, 1, h, False)

            @pl.when(jnp.logical_and(s < z, z == n_strip - 1))
            def _():
                send_sum(s, 0, h, False)

            return c

        lax.fori_loop(0, PARTS, start, 0)
        return carry

    def pass_on(i, carry):
        s = nth(i)

        def one(h, c):
            @pl.when(jnp.logical_and(s > z, has_left))
            def _():
                send_sum(s, 1, h, True)

            @pl.when(jnp.logical_and(s < z, has_right))
            def _():
                send_sum(s, 0, h, True)

            return c

        lax.fori_loop(0, PARTS, one, 0)
        return carry

    last = n_strip - 1

    def sum_step(i, carry):
        @pl.when(i == last)
        def _():
            pass_on(0, 0)
            project_mlp(z)
            lax.fori_loop(1, min(2, last), pass_on, 0)

        cross_strip(i, 0)

        @pl.when(i + 1 < n_strip)
        def _():
            self_strip(i + 1, 0)

        return carry

    lax.fori_loop(0, n_strip, sum_step, 0)
    lax.fori_loop(min(2, last), last, pass_on, 0)

    def finish(h, carry):
        here = pl.ds(pl.multiple_of(h * part, part), part)

        @pl.when(has_left)
        def _():
            rs_copy(0, 1, h, z).wait_recv()
            acc[z, here] = acc[z, here] + rs_recv[z, here].astype(F32)

        @pl.when(has_right)
        def _():
            rs_copy(0, 0, h, n_strip).wait_recv()
            acc[z, here] = acc[z, here] + rs_recv[n_strip, here].astype(F32)

        out[0, here] = (tokens[0, here].astype(F32) + acc[z, here]).astype(BF16)
        return carry

    lax.fori_loop(0, PARTS, finish, 0)

    def settle(t, carry):
        def one(h, c):
            @pl.when(jnp.logical_and(has_left, t >= z))
            def _():
                n_copy(t, 0, h).wait_send()

            @pl.when(jnp.logical_and(has_right, t <= z))
            def _():
                n_copy(t, 1, h).wait_send()

            for o, p in enumerate(peers):
                kv_copy(v, t, h, p, kv_send.at[o, t, h]).wait_send()
                kv_copy(p, t, h, mate, fwd_send.at[o, t, h]).wait_send()
            kv_copy(v, t, h, mate, kv_send.at[n_chip - 1, t, h]).wait_send()

            @pl.when(t > z)
            def _():
                rs_copy(t, 1, h).wait_send()

            @pl.when(t < z)
            def _():
                rs_copy(t, 0, h).wait_send()

            return c

        lax.fori_loop(0, PARTS, one, 0)
        return carry

    lax.fori_loop(0, n_strip, settle, 0)


def per_device(n_view, n_strip, tokens, source_ids, source_count, *weights):
    rows, width = tokens.shape[1:]
    hc = weights[0].shape[1]
    hidden = weights[-2].shape[1]
    slots = source_ids.shape[2]
    up = next(u for u in (768, 512, 256, 128, hidden) if hidden % u == 0)
    n_up = hidden // up
    pair = 2 if hc % LANES == 0 else 1
    n_chip = n_view // 2
    dma = pltpu.SemaphoreType.DMA
    vmem = pl.BlockSpec(memory_space=pltpu.VMEM)
    hbm = pl.BlockSpec(memory_space=pl.ANY)
    return pl.pallas_call(
        functools.partial(kernel, n_view, n_strip, slots),
        out_shape=jax.ShapeDtypeStruct(tokens.shape, tokens.dtype),
        in_specs=[hbm, hbm, vmem] + [hbm] * len(weights),
        out_specs=vmem,
        scratch_shapes=[
            pltpu.SMEM(source_ids.shape[::-1], jnp.int32),
            pltpu.SMEM(source_count.shape[::-1], jnp.int32),
            pltpu.VMEM((6 // pair, width, pair * hc), BF16),
            pltpu.VMEM((2 * hc, width), BF16),
            pltpu.VMEM((n_up, width, up), BF16),
            pltpu.VMEM((n_up, up, width), BF16),
            pltpu.VMEM((n_strip, rows, width), BF16),
            pltpu.VMEM((4, n_strip, rows, hc), BF16),
            pltpu.VMEM((n_view * n_strip, rows, 2 * hc), BF16),
            pltpu.VMEM((slots, rows, 2 * hc), BF16),
            pltpu.VMEM((n_strip, rows, width), F32),
            pltpu.VMEM((n_strip, rows, width), BF16),
            pltpu.VMEM((n_strip + 1, rows, width), BF16),
            dma((10 + 2 * n_up,)),
            dma((2, n_strip, PARTS)),
            dma((n_strip, PARTS)),
            dma((n_chip, n_strip, PARTS)),
            dma((n_chip, n_strip, PARTS)),
            dma((n_view * n_strip, PARTS)),
            dma((n_strip, PARTS)),
            dma((n_strip + 1, PARTS)),
        ],
        compiler_params=pltpu.CompilerParams(
            collective_id=0, has_side_effects=True, vmem_limit_bytes=60 * 1024 * 1024
        ),
    )(source_ids.transpose(2, 1, 0), source_count.T, tokens, *weights)


def solution(mesh):
    column, row = P(None, "strip"), P("strip", None)
    in_specs = (
        P("view", "strip", None),
        P(),
        P(),
        column,
        column,
        column,
        row,
        column,
        column,
        column,
        row,
        column,
        row,
    )
    return jax.shard_map(
        functools.partial(per_device, mesh.shape["view"], mesh.shape["strip"]),
        mesh=mesh,
        in_specs=in_specs,
        out_specs=P("view", "strip", None),
        check_vma=False,
    )
```

```python
import functools
import math

import jax
import jax.numpy as jnp
from jax import lax
from jax.experimental import pallas as pl
from jax.experimental.pallas import tpu as pltpu
from jax.sharding import PartitionSpec as P

HEAD_DIM = 64
LANES = 128
PARTS = 2
SUM_PARTS = 4
MESH = pl.DeviceIdType.MESH
F32 = jnp.float32
BF16 = jnp.bfloat16


def dot(a, b):
    return jnp.dot(a, b, preferred_element_type=F32)


def dot_nt(a, b):
    return lax.dot_general(a, b, (((1,), (1,)), ((), ())), preferred_element_type=F32)


def attend(q, keys, values, bias):
    cols = q.shape[1]
    parts = []
    for lo in range(0, cols, LANES):
        hi = min(lo + LANES, cols)
        q_block = q[:, lo:hi] * jnp.asarray(1.0 / math.sqrt(HEAD_DIM), BF16)
        k_block, v_block = keys(lo, hi), values(lo, hi)
        lane = lax.broadcasted_iota(jnp.int32, q_block.shape, 1)
        heads = (hi - lo) // HEAD_DIM
        inside = [
            jnp.logical_and(lane >= h * HEAD_DIM, lane < (h + 1) * HEAD_DIM) for h in range(heads)
        ]
        stacked = jnp.concatenate([jnp.where(m, q_block, jnp.zeros_like(q_block)) for m in inside])
        scores = dot_nt(stacked, k_block)
        if bias is not None:
            scores = scores + bias
        top = jnp.max(scores, axis=-1, keepdims=True)
        weights = jnp.exp(scores - top)
        total = jnp.sum(weights, axis=-1, keepdims=True)
        mixed = dot(weights.astype(BF16), v_block) * (1.0 / total)
        count = q.shape[0]
        result = mixed[:count]
        for h in range(1, heads):
            result = jnp.where(inside[h], mixed[h * count : (h + 1) * count], result)
        parts.append(result.astype(BF16))
    return parts[0] if len(parts) == 1 else jnp.concatenate(parts, axis=1)


def kernel(
    n_view,
    n_strip,
    slots,
    ids_in,
    counts_in,
    tokens,
    w_sq,
    w_sk,
    w_sv,
    w_so,
    w_cq,
    w_ck,
    w_cv,
    w_co,
    w_up,
    w_down,
    out,
    ids,
    counts,
    wa,
    wo,
    wm,
    md,
    nbuf,
    proj,
    kv,
    kbuf,
    acc,
    rs_send,
    rs_recv,
    w_sem,
    n_send,
    n_recv,
    kv_send,
    fwd_send,
    kv_recv,
    rs_ssem,
    rs_rsem,
):
    v = lax.axis_index("view")
    z = lax.axis_index("strip")
    n_chip = n_view // 2
    chip, core = v // 2, v % 2
    mate = chip * 2 + 1 - core
    rows = tokens.shape[1]
    hc = w_sq.shape[1]
    part = rows // PARTS
    sum_part = rows // SUM_PARTS
    n_up, _, up = wm.shape
    pair = wa.shape[2] // hc
    has_left, has_right = z > 0, z < n_strip - 1

    loads = []

    def load(src, dst):
        copy = pltpu.make_async_copy(src, dst, w_sem.at[len(loads)])
        copy.start()
        loads.append(copy)

    def load_columns(src, i):
        if pair == 2:
            load(src, wa.at[i // 2, :, pl.ds(i % 2 * hc, hc)])
        else:
            load(src, wa.at[i])

    load_columns(w_ck, 4)
    load_columns(w_cv, 5)

    barrier = pltpu.get_barrier_semaphore()

    def greet(view, strip):
        pl.semaphore_signal(barrier, inc=1, device_id=(view, strip), device_id_type=MESH)

    peers = [lax.rem(chip + o, n_chip) * 2 + core for o in range(1, n_chip)]
    for p in peers:
        greet(p, z)
    greet(mate, z)

    @pl.when(has_left)
    def _():
        greet(v, z - 1)

    @pl.when(has_right)
    def _():
        greet(v, z + 1)

    wide = tokens[0].astype(F32)
    nbuf[z] = (wide * lax.rsqrt(jnp.mean(wide * wide, axis=-1, keepdims=True) + 1e-06)).astype(BF16)
    pl.semaphore_wait(
        barrier, len(peers) + 1 + jnp.where(has_left, 1, 0) + jnp.where(has_right, 1, 0)
    )

    def piece(ref, index, h, size=part):
        return ref.at[index, pl.ds(pl.multiple_of(h * size, size), size)]

    def n_copy(b, side, h):
        return pltpu.make_async_remote_copy(
            src_ref=piece(nbuf, b, h),
            dst_ref=piece(nbuf, b, h),
            send_sem=n_send.at[side, b, h],
            recv_sem=n_recv.at[b, h],
            device_id=(v, z + (2 * side - 1)),
            device_id_type=MESH,
        )

    def kv_copy(view, t, h, to, sem):
        index = view * n_strip + t
        return pltpu.make_async_remote_copy(
            src_ref=piece(kv, index, h),
            dst_ref=piece(kv, index, h),
            send_sem=sem,
            recv_sem=kv_recv.at[index, h],
            device_id=(to, z),
            device_id_type=MESH,
        )

    def share(t, h):
        for o, p in enumerate(peers):
            kv_copy(v, t, h, p, kv_send.at[o, t, h]).start()
        kv_copy(v, t, h, mate, kv_send.at[n_chip - 1, t, h]).start()

    def forward(t):
        def one(h, carry):
            for o, p in enumerate(peers):
                kv_copy(p, t, h, mate, fwd_send.at[o, t, h]).wait_recv()
                kv_copy(p, t, h, mate, fwd_send.at[o, t, h]).start()
            return carry

        lax.fori_loop(0, PARTS, one, 0)

    def project_kv(b, h):
        here = pl.ds(pl.multiple_of(h * part, part), part)
        x = nbuf[b, here]
        index = v * n_strip + b
        if pair == 2:
            kv[index, here] = dot(x, wa[2]).astype(BF16)
        else:
            kv[index, here, 0:hc] = dot(x, wa[4]).astype(BF16)
            kv[index, here, hc : 2 * hc] = dot(x, wa[5]).astype(BF16)
        share(b, h)

    def project_qkv(b):
        def one(i, carry):
            product = dot(nbuf[b], wa[i]).astype(BF16)
            for half in range(pair):
                proj[pair * i + half, b] = product[:, half * hc : (half + 1) * hc]
            return carry

        lax.fori_loop(0, 4 // pair, one, 0)

    def project_mlp(b):
        def mlp(j, carry):
            hidden = jax.nn.gelu(dot(nbuf[b], wm[j])).astype(BF16)
            term = dot(hidden, md[j])

            @pl.when(j == 0)
            def _():
                acc[b] = term

            @pl.when(j > 0)
            def _():
                acc[b] = acc[b] + term

            return carry

        lax.fori_loop(0, n_up, mlp, 0)

    def at_distance(d, fn):
        @pl.when(z - d >= 0)
        def _():
            fn(z - d)

        @pl.when(jnp.logical_and(z + d < n_strip, d > 0))
        def _():
            fn(z + d)

    for h in range(PARTS):

        @pl.when(has_left)
        def _():
            n_copy(z, 0, h).start()

        @pl.when(has_right)
        def _():
            n_copy(z, 1, h).start()

    load_columns(w_sq, 0)
    load_columns(w_sk, 1)
    load_columns(w_sv, 2)
    load_columns(w_cq, 3)
    for j in range(n_up):
        load(w_up.at[:, pl.ds(j * up, up)], wm.at[j])
    for j in range(n_up):
        load(w_down.at[pl.ds(j * up, up)], md.at[j])
    load(w_so, wo.at[pl.ds(0, hc)])
    load(w_co, wo.at[pl.ds(hc, hc)])
    load(ids_in, ids)
    load(counts_in, counts)

    for copy in loads[:2]:
        copy.wait()

    def own_kv(h, carry):
        project_kv(z, h)
        return carry

    lax.fori_loop(0, PARTS, own_kv, 0)
    for copy in loads[2:]:
        copy.wait()
    project_qkv(z)

    def gather_step(d, carry):
        def one(fn):
            def side_step(side, c):
                b = z + (2 * side - 1) * d

                @pl.when(jnp.logical_and(b >= 0, b < n_strip))
                def _():
                    fn(b)

                return c

            lax.fori_loop(0, 2, side_step, 0)

        def arrive(h, c):
            @pl.when(z - d >= 0)
            def _():
                n_copy(z - d, 1, h).wait_recv()

                @pl.when(has_right)
                def _():
                    n_copy(z - d, 1, h).start()

            @pl.when(z + d < n_strip)
            def _():
                n_copy(z + d, 0, h).wait_recv()

                @pl.when(has_left)
                def _():
                    n_copy(z + d, 0, h).start()

            one(lambda b: project_kv(b, h))

            late = z + (2 * h - 1) * (d - 1)

            @pl.when((h < 2) & (d > 1) & (late >= 0) & (late < n_strip))
            def _():
                project_mlp(late)

            return c

        lax.fori_loop(0, PARTS, arrive, 0)
        one(project_qkv)
        at_distance(d - 1, forward)
        return carry

    lax.fori_loop(1, n_strip, gather_step, 0)

    def nth(i):
        if n_strip > 2:
            i = jnp.where(i < 2, 1 - i, i)
        low = n_strip - 1 - i
        low = jnp.where(low > z, low, low - 1)
        high = jnp.where(i < z, i, i + 1)
        return jnp.where(i == n_strip - 1, z, jnp.where(z < n_strip // 2, low, high))

    def self_strip(i, carry):
        s = nth(i)

        def columns(i):
            return lambda lo, hi: proj[i, :, :, lo:hi].reshape(n_strip * rows, hi - lo)

        proj[0, s] = attend(proj[0, s], columns(1), columns(2), None)
        return carry

    def self_first(i, carry):
        self_strip(i, 0)

        @pl.when(i == 0)
        def _():
            at_distance(n_strip - 1, forward)

        return carry

    lax.fori_loop(0, 2, self_first, 0)

    def from_mate(t, carry):
        def one(h, c):
            kv_copy(mate, t, h, mate, fwd_send.at[0, t, h]).wait_recv()
            for p in peers:
                kv_copy(p + 1 - 2 * core, t, h, mate, fwd_send.at[0, t, h]).wait_recv()
            return c

        lax.fori_loop(0, PARTS, one, 0)
        return carry

    lax.fori_loop(0, n_strip, from_mate, 0)

    def rs_copy(s, side, h, slot=None):
        if slot is None:
            slot = jnp.where(jnp.logical_and(side == 0, s == z - 1), n_strip, s)
        return pltpu.make_async_remote_copy(
            src_ref=piece(rs_send, s, h, sum_part),
            dst_ref=piece(rs_recv, slot, h, sum_part),
            send_sem=rs_ssem.at[s, h],
            recv_sem=rs_rsem.at[slot, h],
            device_id=(v, z + (2 * side - 1)),
            device_id_type=MESH,
        )

    def send_sum(s, side, h, arrived):
        here = pl.ds(pl.multiple_of(h * sum_part, sum_part), sum_part)
        total = acc[s, here]
        if arrived:
            rs_copy(0, side, h, s).wait_recv()
            total = total + rs_recv[s, here].astype(F32)
        rs_send[s, here] = total.astype(BF16)
        rs_copy(s, side, h).start()

    def cross_strip(i, carry):
        s = nth(i)
        for k in range(slots):
            kbuf[k] = kv[ids[k, s, v]]
        count = counts[s, v]
        column = lax.broadcasted_iota(jnp.int32, (1, slots * rows), 1)
        bias = jnp.where(column < count * rows, 0.0, -1e30).astype(F32)

        def columns(start):
            return lambda lo, hi: kbuf[:, :, start + lo : start + hi].reshape(slots * rows, hi - lo)

        mixed = attend(proj[3, s], columns(0), columns(hc), bias)
        acc[s] = acc[s] + dot(jnp.concatenate([proj[0, s], mixed], axis=1), wo[...])

        def start(h, c):
            @pl.when(jnp.logical_and(s > z, z == 0))
            def _():
                send_sum(s, 1, h, False)

            @pl.when(jnp.logical_and(s < z, z == n_strip - 1))
            def _():
                send_sum(s, 0, h, False)

            return c

        lax.fori_loop(0, SUM_PARTS, start, 0)
        return carry

    def pass_on(i, carry):
        s = nth(i)

        def one(h, c):
            @pl.when(jnp.logical_and(s > z, has_left))
            def _():
                send_sum(s, 1, h, True)

            @pl.when(jnp.logical_and(s < z, has_right))
            def _():
                send_sum(s, 0, h, True)

            return c

        lax.fori_loop(0, SUM_PARTS, one, 0)
        return carry

    last = n_strip - 1

    def sum_step(i, carry):
        @pl.when(i == last)
        def _():
            pass_on(0, 0)
            project_mlp(z)
            lax.fori_loop(1, min(2, last), pass_on, 0)

        cross_strip(i, 0)

        @pl.when(i == 0)
        def _():
            at_distance(n_strip - 1, project_mlp)

        @pl.when(i + 2 < n_strip)
        def _():
            self_strip(i + 2, 0)

        return carry

    lax.fori_loop(0, n_strip, sum_step, 0)
    lax.fori_loop(min(2, last), last, pass_on, 0)

    def finish(h, carry):
        here = pl.ds(pl.multiple_of(h * sum_part, sum_part), sum_part)

        @pl.when(has_left)
        def _():
            rs_copy(0, 1, h, z).wait_recv()
            acc[z, here] = acc[z, here] + rs_recv[z, here].astype(F32)

        @pl.when(has_right)
        def _():
            rs_copy(0, 0, h, n_strip).wait_recv()
            acc[z, here] = acc[z, here] + rs_recv[n_strip, here].astype(F32)

        out[0, here] = (tokens[0, here].astype(F32) + acc[z, here]).astype(BF16)
        return carry

    lax.fori_loop(0, SUM_PARTS, finish, 0)

    def settle(t, carry):
        def one(h, c):
            @pl.when(jnp.logical_and(has_left, t >= z))
            def _():
                n_copy(t, 0, h).wait_send()

            @pl.when(jnp.logical_and(has_right, t <= z))
            def _():
                n_copy(t, 1, h).wait_send()

            for o, p in enumerate(peers):
                kv_copy(v, t, h, p, kv_send.at[o, t, h]).wait_send()
                kv_copy(p, t, h, mate, fwd_send.at[o, t, h]).wait_send()
            kv_copy(v, t, h, mate, kv_send.at[n_chip - 1, t, h]).wait_send()

            return c

        def one_sum(h, c):
            @pl.when(t > z)
            def _():
                rs_copy(t, 1, h).wait_send()

            @pl.when(t < z)
            def _():
                rs_copy(t, 0, h).wait_send()

            return c

        lax.fori_loop(0, PARTS, one, 0)
        lax.fori_loop(0, SUM_PARTS, one_sum, 0)
        return carry

    lax.fori_loop(0, n_strip, settle, 0)


def per_device(n_view, n_strip, tokens, source_ids, source_count, *weights):
    rows, width = tokens.shape[1:]
    hc = weights[0].shape[1]
    hidden = weights[-2].shape[1]
    slots = source_ids.shape[2]
    up = next(u for u in (768, 512, 256, 128, hidden) if hidden % u == 0)
    n_up = hidden // up
    pair = 2 if hc % LANES == 0 else 1
    n_chip = n_view // 2
    dma = pltpu.SemaphoreType.DMA
    vmem = pl.BlockSpec(memory_space=pltpu.VMEM)
    hbm = pl.BlockSpec(memory_space=pl.ANY)
    return pl.pallas_call(
        functools.partial(kernel, n_view, n_strip, slots),
        out_shape=jax.ShapeDtypeStruct(tokens.shape, tokens.dtype),
        in_specs=[hbm, hbm, vmem] + [hbm] * len(weights),
        out_specs=vmem,
        scratch_shapes=[
            pltpu.SMEM(source_ids.shape[::-1], jnp.int32),
            pltpu.SMEM(source_count.shape[::-1], jnp.int32),
            pltpu.VMEM((6 // pair, width, pair * hc), BF16),
            pltpu.VMEM((2 * hc, width), BF16),
            pltpu.VMEM((n_up, width, up), BF16),
            pltpu.VMEM((n_up, up, width), BF16),
            pltpu.VMEM((n_strip, rows, width), BF16),
            pltpu.VMEM((4, n_strip, rows, hc), BF16),
            pltpu.VMEM((n_view * n_strip, rows, 2 * hc), BF16),
            pltpu.VMEM((slots, rows, 2 * hc), BF16),
            pltpu.VMEM((n_strip, rows, width), F32),
            pltpu.VMEM((n_strip, rows, width), BF16),
            pltpu.VMEM((n_strip + 1, rows, width), BF16),
            dma((10 + 2 * n_up,)),
            dma((2, n_strip, PARTS)),
            dma((n_strip, PARTS)),
            dma((n_chip, n_strip, PARTS)),
            dma((n_chip, n_strip, PARTS)),
            dma((n_view * n_strip, PARTS)),
            dma((n_strip, SUM_PARTS)),
            dma((n_strip + 1, SUM_PARTS)),
        ],
        compiler_params=pltpu.CompilerParams(
            collective_id=0, has_side_effects=True, vmem_limit_bytes=60 * 1024 * 1024
        ),
    )(source_ids.transpose(2, 1, 0), source_count.T, tokens, *weights)


def solution(mesh):
    column, row = P(None, "strip"), P("strip", None)
    in_specs = (
        P("view", "strip", None),
        P(),
        P(),
        column,
        column,
        column,
        row,
        column,
        column,
        column,
        row,
        column,
        row,
    )
    return jax.shard_map(
        functools.partial(per_device, mesh.shape["view"], mesh.shape["strip"]),
        mesh=mesh,
        in_specs=in_specs,
        out_specs=P("view", "strip", None),
        check_vma=False,
    )
```

```python
import functools
import math

import jax
import jax.numpy as jnp
from jax import lax
from jax.experimental import pallas as pl
from jax.experimental.pallas import tpu as pltpu
from jax.sharding import PartitionSpec as P

HEAD_DIM = 64
LANES = 128
PARTS = 2
SUM_PARTS = 4
MESH = pl.DeviceIdType.MESH
F32 = jnp.float32
BF16 = jnp.bfloat16


def dot(a, b):
    return jnp.dot(a, b, preferred_element_type=F32)


def dot_nt(a, b):
    return lax.dot_general(a, b, (((1,), (1,)), ((), ())), preferred_element_type=F32)


def attend(q, keys, values, bias):
    cols = q.shape[1]
    parts = []
    for lo in range(0, cols, LANES):
        hi = min(lo + LANES, cols)
        q_block = q[:, lo:hi] * jnp.asarray(1.0 / math.sqrt(HEAD_DIM), BF16)
        k_block, v_block = keys(lo, hi), values(lo, hi)
        lane = lax.broadcasted_iota(jnp.int32, q_block.shape, 1)
        heads = (hi - lo) // HEAD_DIM
        inside = [
            jnp.logical_and(lane >= h * HEAD_DIM, lane < (h + 1) * HEAD_DIM) for h in range(heads)
        ]
        stacked = jnp.concatenate([jnp.where(m, q_block, jnp.zeros_like(q_block)) for m in inside])
        scores = dot_nt(stacked, k_block)
        if bias is not None:
            scores = scores + bias
        top = jnp.max(scores, axis=-1, keepdims=True)
        weights = jnp.exp(scores - top)
        total = jnp.sum(weights, axis=-1, keepdims=True)
        mixed = dot(weights.astype(BF16), v_block) * (1.0 / total)
        count = q.shape[0]
        result = mixed[:count]
        for h in range(1, heads):
            result = jnp.where(inside[h], mixed[h * count : (h + 1) * count], result)
        parts.append(result.astype(BF16))
    return parts[0] if len(parts) == 1 else jnp.concatenate(parts, axis=1)


def kernel(
    n_view,
    n_strip,
    slots,
    ids_in,
    counts_in,
    tokens,
    w_sq,
    w_sk,
    w_sv,
    w_so,
    w_cq,
    w_ck,
    w_cv,
    w_co,
    w_up,
    w_down,
    out,
    ids,
    counts,
    wa,
    wo,
    wm,
    md,
    nbuf,
    proj,
    kv,
    kbuf,
    acc,
    rs_send,
    rs_recv,
    w_sem,
    n_send,
    n_recv,
    kv_send,
    fwd_send,
    kv_recv,
    rs_ssem,
    rs_rsem,
):
    v = lax.axis_index("view")
    z = lax.axis_index("strip")
    n_chip = n_view // 2
    chip, core = v // 2, v % 2
    mate = chip * 2 + 1 - core
    rows = tokens.shape[1]
    hc = w_sq.shape[1]
    part = rows // PARTS
    sum_part = rows // SUM_PARTS
    n_up, _, up = wm.shape
    pair = wa.shape[2] // hc
    has_left, has_right = z > 0, z < n_strip - 1

    loads = []

    def load(src, dst):
        copy = pltpu.make_async_copy(src, dst, w_sem.at[len(loads)])
        copy.start()
        loads.append(copy)

    def load_columns(src, i):
        if pair == 2:
            load(src, wa.at[i // 2, :, pl.ds(i % 2 * hc, hc)])
        else:
            load(src, wa.at[i])

    load_columns(w_ck, 4)
    load_columns(w_cv, 5)

    barrier = pltpu.get_barrier_semaphore()

    def greet(view, strip):
        pl.semaphore_signal(barrier, inc=1, device_id=(view, strip), device_id_type=MESH)

    peers = [lax.rem(chip + o, n_chip) * 2 + core for o in range(1, n_chip)]
    for p in peers:
        greet(p, z)
    greet(mate, z)

    @pl.when(has_left)
    def _():
        greet(v, z - 1)

    @pl.when(has_right)
    def _():
        greet(v, z + 1)

    wide = tokens[0].astype(F32)
    nbuf[z] = (wide * lax.rsqrt(jnp.mean(wide * wide, axis=-1, keepdims=True) + 1e-06)).astype(BF16)
    pl.semaphore_wait(
        barrier, len(peers) + 1 + jnp.where(has_left, 1, 0) + jnp.where(has_right, 1, 0)
    )

    def piece(ref, index, h, size=part):
        return ref.at[index, pl.ds(pl.multiple_of(h * size, size), size)]

    def n_copy(b, side, h):
        return pltpu.make_async_remote_copy(
            src_ref=piece(nbuf, b, h),
            dst_ref=piece(nbuf, b, h),
            send_sem=n_send.at[side, b, h],
            recv_sem=n_recv.at[b, h],
            device_id=(v, z + (2 * side - 1)),
            device_id_type=MESH,
        )

    def kv_copy(view, t, h, to, sem):
        index = view * n_strip + t
        return pltpu.make_async_remote_copy(
            src_ref=piece(kv, index, h),
            dst_ref=piece(kv, index, h),
            send_sem=sem,
            recv_sem=kv_recv.at[index, h],
            device_id=(to, z),
            device_id_type=MESH,
        )

    def share(t, h):
        for o, p in enumerate(peers):
            kv_copy(v, t, h, p, kv_send.at[o, t, h]).start()
        kv_copy(v, t, h, mate, kv_send.at[n_chip - 1, t, h]).start()

    def forward(t):
        def one(h, carry):
            for o, p in enumerate(peers):
                kv_copy(p, t, h, mate, fwd_send.at[o, t, h]).wait_recv()
                kv_copy(p, t, h, mate, fwd_send.at[o, t, h]).start()
            return carry

        lax.fori_loop(0, PARTS, one, 0)

    def project_kv(b, h):
        here = pl.ds(pl.multiple_of(h * part, part), part)
        x = nbuf[b, here]
        index = v * n_strip + b
        if pair == 2:
            kv[index, here] = dot(x, wa[2]).astype(BF16)
        else:
            kv[index, here, 0:hc] = dot(x, wa[4]).astype(BF16)
            kv[index, here, hc : 2 * hc] = dot(x, wa[5]).astype(BF16)
        share(b, h)

    def project_qkv(b):
        def one(i, carry):
            product = dot(nbuf[b], wa[i]).astype(BF16)
            for half in range(pair):
                proj[pair * i + half, b] = product[:, half * hc : (half + 1) * hc]
            return carry

        lax.fori_loop(0, 4 // pair, one, 0)

    def project_mlp(b):
        def mlp(j, carry):
            hidden = jax.nn.gelu(dot(nbuf[b], wm[j])).astype(BF16)
            term = dot(hidden, md[j])

            @pl.when(j == 0)
            def _():
                acc[b] = term

            @pl.when(j > 0)
            def _():
                acc[b] = acc[b] + term

            return carry

        lax.fori_loop(0, n_up, mlp, 0)

    def at_distance(d, fn):
        @pl.when(z - d >= 0)
        def _():
            fn(z - d)

        @pl.when(jnp.logical_and(z + d < n_strip, d > 0))
        def _():
            fn(z + d)

    for h in range(PARTS):

        @pl.when(has_left)
        def _():
            n_copy(z, 0, h).start()

        @pl.when(has_right)
        def _():
            n_copy(z, 1, h).start()

    load_columns(w_sq, 0)
    load_columns(w_sk, 1)
    load_columns(w_sv, 2)
    load_columns(w_cq, 3)
    for j in range(n_up):
        load(w_up.at[:, pl.ds(j * up, up)], wm.at[j])
    for j in range(n_up):
        load(w_down.at[pl.ds(j * up, up)], md.at[j])
    load(w_so, wo.at[pl.ds(0, hc)])
    load(w_co, wo.at[pl.ds(hc, hc)])
    load(ids_in, ids)
    load(counts_in, counts)

    for copy in loads[:2]:
        copy.wait()

    def own_kv(h, carry):
        project_kv(z, h)
        return carry

    lax.fori_loop(0, PARTS, own_kv, 0)
    for copy in loads[2:]:
        copy.wait()
    project_qkv(z)

    def gather_step(d, carry):
        def one(fn):
            def side_step(side, c):
                b = z + (2 * side - 1) * d

                @pl.when(jnp.logical_and(b >= 0, b < n_strip))
                def _():
                    fn(b)

                return c

            lax.fori_loop(0, 2, side_step, 0)

        def arrive(h, c):
            @pl.when(z - d >= 0)
            def _():
                n_copy(z - d, 1, h).wait_recv()

                @pl.when(has_right)
                def _():
                    n_copy(z - d, 1, h).start()

            @pl.when(z + d < n_strip)
            def _():
                n_copy(z + d, 0, h).wait_recv()

                @pl.when(has_left)
                def _():
                    n_copy(z + d, 0, h).start()

            one(lambda b: project_kv(b, h))

            late = z + (2 * h - 1) * (d - 1)

            @pl.when((h < 2) & (d > 1) & (late >= 0) & (late < n_strip))
            def _():
                project_mlp(late)

            return c

        lax.fori_loop(0, PARTS, arrive, 0)
        one(project_qkv)
        at_distance(d - 1, forward)
        return carry

    lax.fori_loop(1, n_strip, gather_step, 0)

    def nth(i):
        if n_strip > 2:
            i = jnp.where(i < 2, 1 - i, i)
        low = n_strip - 1 - i
        low = jnp.where(low > z, low, low - 1)
        high = jnp.where(i < z, i, i + 1)
        return jnp.where(i == n_strip - 1, z, jnp.where(z < n_strip // 2, low, high))

    def self_strip(i, carry):
        s = nth(i)

        def columns(i):
            return lambda lo, hi: proj[i, :, :, lo:hi].reshape(n_strip * rows, hi - lo)

        proj[0, s] = attend(proj[0, s], columns(1), columns(2), None)
        return carry

    def self_first(i, carry):
        self_strip(i, 0)

        @pl.when(i == 0)
        def _():
            at_distance(n_strip - 1, forward)

        return carry

    lax.fori_loop(0, 2, self_first, 0)

    def from_mate(t, carry):
        def one(h, c):
            kv_copy(mate, t, h, mate, fwd_send.at[0, t, h]).wait_recv()
            for p in peers:
                kv_copy(p + 1 - 2 * core, t, h, mate, fwd_send.at[0, t, h]).wait_recv()
            return c

        lax.fori_loop(0, PARTS, one, 0)
        return carry

    lax.fori_loop(0, n_strip, from_mate, 0)

    def rs_copy(s, side, h, slot=None):
        if slot is None:
            slot = jnp.where(jnp.logical_and(side == 0, s == z - 1), n_strip, s)
        return pltpu.make_async_remote_copy(
            src_ref=piece(rs_send, s, h, sum_part),
            dst_ref=piece(rs_recv, slot, h, sum_part),
            send_sem=rs_ssem.at[s, h],
            recv_sem=rs_rsem.at[slot, h],
            device_id=(v, z + (2 * side - 1)),
            device_id_type=MESH,
        )

    def send_sum(s, side, h, arrived):
        here = pl.ds(pl.multiple_of(h * sum_part, sum_part), sum_part)
        total = acc[s, here]
        if arrived:
            rs_copy(0, side, h, s).wait_recv()
            total = total + rs_recv[s, here].astype(F32)
        rs_send[s, here] = total.astype(BF16)
        rs_copy(s, side, h).start()

    def cross_strip(i, carry):
        s = nth(i)
        for k in range(slots):
            kbuf[k] = kv[ids[k, s, v]]
        count = counts[s, v]
        column = lax.broadcasted_iota(jnp.int32, (1, slots * rows), 1)
        bias = jnp.where(column < count * rows, 0.0, -1e30).astype(F32)

        def columns(start):
            return lambda lo, hi: kbuf[:, :, start + lo : start + hi].reshape(slots * rows, hi - lo)

        mixed = attend(proj[3, s], columns(0), columns(hc), bias)
        acc[s] = acc[s] + dot(jnp.concatenate([proj[0, s], mixed], axis=1), wo[...])

        def start(h, c):
            @pl.when(jnp.logical_and(s > z, z == 0))
            def _():
                send_sum(s, 1, h, False)

            @pl.when(jnp.logical_and(s < z, z == n_strip - 1))
            def _():
                send_sum(s, 0, h, False)

            return c

        lax.fori_loop(0, SUM_PARTS, start, 0)
        return carry

    def pass_on(i, carry):
        s = nth(i)

        def one(h, c):
            @pl.when(jnp.logical_and(s > z, has_left))
            def _():
                send_sum(s, 1, h, True)

            @pl.when(jnp.logical_and(s < z, has_right))
            def _():
                send_sum(s, 0, h, True)

            return c

        lax.fori_loop(0, SUM_PARTS, one, 0)
        return carry

    last = n_strip - 1

    def sum_step(i, carry):
        @pl.when(i == max(last - 1, 1))
        def _():
            pass_on(0, 0)

        @pl.when(i == last)
        def _():
            project_mlp(z)
            lax.fori_loop(1, min(2, last), pass_on, 0)

        cross_strip(i, 0)

        @pl.when(i == 0)
        def _():
            at_distance(n_strip - 1, project_mlp)

        @pl.when(i + 2 < n_strip)
        def _():
            self_strip(i + 2, 0)

        return carry

    lax.fori_loop(0, n_strip, sum_step, 0)
    lax.fori_loop(min(2, last), last, pass_on, 0)

    def finish(h, carry):
        here = pl.ds(pl.multiple_of(h * sum_part, sum_part), sum_part)

        @pl.when(has_left)
        def _():
            rs_copy(0, 1, h, z).wait_recv()
            acc[z, here] = acc[z, here] + rs_recv[z, here].astype(F32)

        @pl.when(has_right)
        def _():
            rs_copy(0, 0, h, n_strip).wait_recv()
            acc[z, here] = acc[z, here] + rs_recv[n_strip, here].astype(F32)

        out[0, here] = (tokens[0, here].astype(F32) + acc[z, here]).astype(BF16)
        return carry

    lax.fori_loop(0, SUM_PARTS, finish, 0)

    def settle(t, carry):
        def one(h, c):
            @pl.when(jnp.logical_and(has_left, t >= z))
            def _():
                n_copy(t, 0, h).wait_send()

            @pl.when(jnp.logical_and(has_right, t <= z))
            def _():
                n_copy(t, 1, h).wait_send()

            for o, p in enumerate(peers):
                kv_copy(v, t, h, p, kv_send.at[o, t, h]).wait_send()
                kv_copy(p, t, h, mate, fwd_send.at[o, t, h]).wait_send()
            kv_copy(v, t, h, mate, kv_send.at[n_chip - 1, t, h]).wait_send()

            return c

        def one_sum(h, c):
            @pl.when(t > z)
            def _():
                rs_copy(t, 1, h).wait_send()

            @pl.when(t < z)
            def _():
                rs_copy(t, 0, h).wait_send()

            return c

        lax.fori_loop(0, PARTS, one, 0)
        lax.fori_loop(0, SUM_PARTS, one_sum, 0)
        return carry

    lax.fori_loop(0, n_strip, settle, 0)


def per_device(n_view, n_strip, tokens, source_ids, source_count, *weights):
    rows, width = tokens.shape[1:]
    hc = weights[0].shape[1]
    hidden = weights[-2].shape[1]
    slots = source_ids.shape[2]
    up = next(u for u in (768, 512, 256, 128, hidden) if hidden % u == 0)
    n_up = hidden // up
    pair = 2 if hc % LANES == 0 else 1
    n_chip = n_view // 2
    dma = pltpu.SemaphoreType.DMA
    vmem = pl.BlockSpec(memory_space=pltpu.VMEM)
    hbm = pl.BlockSpec(memory_space=pl.ANY)
    return pl.pallas_call(
        functools.partial(kernel, n_view, n_strip, slots),
        out_shape=jax.ShapeDtypeStruct(tokens.shape, tokens.dtype),
        in_specs=[hbm, hbm, vmem] + [hbm] * len(weights),
        out_specs=vmem,
        scratch_shapes=[
            pltpu.SMEM(source_ids.shape[::-1], jnp.int32),
            pltpu.SMEM(source_count.shape[::-1], jnp.int32),
            pltpu.VMEM((6 // pair, width, pair * hc), BF16),
            pltpu.VMEM((2 * hc, width), BF16),
            pltpu.VMEM((n_up, width, up), BF16),
            pltpu.VMEM((n_up, up, width), BF16),
            pltpu.VMEM((n_strip, rows, width), BF16),
            pltpu.VMEM((4, n_strip, rows, hc), BF16),
            pltpu.VMEM((n_view * n_strip, rows, 2 * hc), BF16),
            pltpu.VMEM((slots, rows, 2 * hc), BF16),
            pltpu.VMEM((n_strip, rows, width), F32),
            pltpu.VMEM((n_strip, rows, width), BF16),
            pltpu.VMEM((n_strip + 1, rows, width), BF16),
            dma((10 + 2 * n_up,)),
            dma((2, n_strip, PARTS)),
            dma((n_strip, PARTS)),
            dma((n_chip, n_strip, PARTS)),
            dma((n_chip, n_strip, PARTS)),
            dma((n_view * n_strip, PARTS)),
            dma((n_strip, SUM_PARTS)),
            dma((n_strip + 1, SUM_PARTS)),
        ],
        compiler_params=pltpu.CompilerParams(
            collective_id=0, has_side_effects=True, vmem_limit_bytes=60 * 1024 * 1024
        ),
    )(source_ids.transpose(2, 1, 0), source_count.T, tokens, *weights)


def solution(mesh):
    column, row = P(None, "strip"), P("strip", None)
    in_specs = (
        P("view", "strip", None),
        P(),
        P(),
        column,
        column,
        column,
        row,
        column,
        column,
        column,
        row,
        column,
        row,
    )
    return jax.shard_map(
        functools.partial(per_device, mesh.shape["view"], mesh.shape["strip"]),
        mesh=mesh,
        in_specs=in_specs,
        out_specs=P("view", "strip", None),
        check_vma=False,
    )
```
